32 devices in a mesh: parts: 2 (over y), expert: 4 (over x, core), cuts: 4 (over z).
Axes of the slice: x: 2, y: 2, z: 4, core: 2. Of those that a mesh axis runs over, the one named last changes fastest.
Arguments:
- inputs: bfloat16 [1536, 3072], P(('parts', 'expert'), 'cuts'), parts along dimension 0, may hold values from -6 to 6
- out_grad: bfloat16 [1536, 3072], P(('parts', 'expert'), 'cuts'), parts along dimension 0, may hold values from -6 to 6
- experts: int32 [1536, 2], P(('parts', 'expert')), parts along dimension 0, may hold values from 0 to 7, all different within a row; in each aligned block of 192 rows (0 to 191, 192 to 383, ...) at most 64 rows name the same one
- route_gates: float32 [1536, 2], P(('parts', 'expert')), parts along dimension 0, may hold values from 0.1 to 0.9
- gate_proj: bfloat16 [8, 3072, 8192], P('expert', None, 'cuts'), may hold values from -0.109375 to 0.109375
- up_proj: bfloat16 [8, 3072, 8192], P('expert', None, 'cuts'), may hold values from -0.109375 to 0.109375
- down_proj: bfloat16 [8, 8192, 3072], P('expert', 'cuts'), may hold values from -0.0625 to 0.0625
- gate_in: bfloat16 [8, 16, 3072], P('expert', None, 'cuts'), may hold values from -0.109375 to 0.109375
- gate_out: bfloat16 [8, 16, 8192], P('expert', None, 'cuts'), may hold values from -0.59765625 to 0.59765625
- up_in: bfloat16 [8, 16, 3072], P('expert', None, 'cuts'), may hold values from -0.109375 to 0.109375
- up_out: bfloat16 [8, 16, 8192], P('expert', None, 'cuts'), may hold values from -0.59765625 to 0.59765625
- down_in: bfloat16 [8, 16, 8192], P('expert', None, 'cuts'), may hold values from -0.0625 to 0.0625
- down_out: bfloat16 [8, 16, 3072], P('expert', None, 'cuts'), may hold values from -0.59765625 to 0.59765625
Outputs:
- input_grad: bfloat16 [1536, 3072], P(('parts', 'expert'), 'cuts'), parts along dimension 0
- grad_gate_in: float32 [16, 16, 3072], P(('parts', 'expert'), None, 'cuts'), parts along dimension 0
- gate_output_gradient: float32 [16, 16, 8192], P(('parts', 'expert'), None, 'cuts'), parts along dimension 0
- grad_up_in: float32 [16, 16, 3072], P(('parts', 'expert'), None, 'cuts'), parts along dimension 0
- up_output_gradient: float32 [16, 16, 8192], P(('parts', 'expert'), None, 'cuts'), parts along dimension 0
- down_input_gradient: float32 [16, 16, 8192], P(('parts', 'expert'), None, 'cuts'), parts along dimension 0
- grad_down_out: float32 [16, 16, 3072], P(('parts', 'expert'), None, 'cuts'), parts along dimension 0
The draws below stay inside these ranges and needn't reach their ends.
There are 2 independent parts, one for each index of `parts`. The reference program is written for one: setup_inputs(seed, part) draws one part's arguments, and reference() takes and returns one part's arrays. A program takes and returns all parts, laid end to end along the dimension named above; an argument that names none is the same for every part. Nothing has to cross between parts.
Inputs may be any that keep to these rules, and one draw needn't show every extreme that they name: Each token names two different experts; among the 192 tokens of one index of expert (aligned blocks of 192 rows) no expert is named more than 64 times.
All inputs are finite; a program needn't handle non-finite values.
Results may differ from the reference program's by a relative error of at most 0.012.
Values may be sent and summed in bfloat16 or wider, within the bound.
No kernel may reach another device: no remote copies, remote signals or barrier semaphores. Data moves between devices by JAX's collectives and lax.ppermute only.
A program may use at most 256 MiB of HBM per device.

```python
import math
import jax
import jax.numpy as jnp
import numpy as np
from jax import lax

D = 3072
FF = 8192
EXPERTS = 8
RANK = 16
TOK_DEV = 192
SLOT = 64
TOKENS = 768
N_EXPERT = 4
N_CUTS = 4


def steps_of(rng, dims, pieces, low, top_value):
    def one(axis_at, parts):
        draws = jax.random.uniform(jax.random.fold_in(jax.random.fold_in(rng, 6), axis_at), (parts,), jnp.float32, low / len(pieces), top_value / len(pieces))
        return jnp.repeat(jnp.exp(draws), dims[axis_at] // parts).reshape((-1,) + (1,) * (len(dims) - axis_at - 1))

    gain = one(*pieces[0])
    for cut in pieces[1:]:
        gain = gain * one(*cut)
    return gain


def assign_block(rng, own, number, rows, amount, top, reach, slope):
    sequence = jax.random.permutation(rng, amount)
    packed, common = shares(amount, rows * top, reach, slope, True), shares(amount, rows * top, reach, slope, False)
    places = jnp.arange(amount)

    def named(lengths, turn):
        used = int((lengths > 0).sum())
        fixed = max(1, used // 4)
        moved = fixed + (places - fixed + turn * (used - fixed)) % max(1, amount - fixed)
        return jnp.zeros((amount,), jnp.int32).at[sequence[jnp.where(places < fixed, places, moved)]].set(jnp.asarray(lengths, jnp.int32))

    lengths = jnp.where(number % 4 == 0, named(packed, number // 4), named(common, number - number // 4 - 1))
    mixed = jax.random.permutation(jax.random.fold_in(own, 3), amount)
    donor, taker = mixed[0:amount // 2 * 2:2], mixed[1:amount // 2 * 2:2]
    margin = jnp.minimum(lengths[donor] - 1, reach - lengths[taker]) // 2
    margin = jnp.where((donor == sequence[0]) | (taker == sequence[0]) | (lengths[taker] == 0), 0, jnp.maximum(margin, 0))
    moved = jax.random.randint(jax.random.fold_in(own, 4), (amount // 2,), 0, 1 << 20) % (margin + 1)
    lengths = lengths.at[donor].add(-moved).at[taker].add(moved)
    items = jnp.searchsorted(jnp.cumsum(lengths), jnp.arange(rows * top), side="right").astype(jnp.int32)
    listing = items.reshape(top, rows).T
    listing = listing[jax.random.permutation(jax.random.fold_in(own, 1), rows)]
    turn = jax.random.randint(jax.random.fold_in(own, 2), (rows, 1), 0, top)
    return jnp.take_along_axis(listing, (jnp.arange(top)[None, :] + turn) % top, axis=1)


def shares(count, total, limit, skew, full):
    weights = [(1 << 20) // math.isqrt(rank ** skew) + 1 for rank in range(1, count + 1)]
    largest = limit if full else min(limit, max(-(-total // count), total * weights[0] // sum(weights)))
    least = 1 if total - largest >= count - 1 else 0
    given, spare = [largest] + [least] * (count - 1), total - largest - least * (count - 1)
    while spare > 0:
        free = [i for i in range(1, count) if given[i] < largest] or [i for i in range(1, count) if given[i] < limit]
        whole, left = sum([weights[i] for i in free]), spare
        for i in free:
            extra = min(limit - given[i], max(1, left * weights[i] // whole), spare)
            given[i] = given[i] + extra
            spare = spare - extra
    return np.array(given)


def bell_draw(key, shape, width, reach, split=(), kind=jnp.bfloat16):
    drawn = jax.random.normal(key, shape, jnp.float32) * width
    if len(split) > 0:
        drawn = steps_of(key, shape, split, -0.22, 0.18) * drawn
    return jnp.clip(drawn, min=-reach, max=reach).astype(kind)


def setup_inputs(seed: int = 0, part: int = 0) -> dict:
    key_of = jax.random.split(jax.random.key(seed), 14)
    part_splits = jax.random.split(jax.random.fold_in(key_of[13], part), 14)
    inputs = bell_draw(part_splits[0], (TOKENS, D), 1.0, 6.0, ((0, 4), (1, 4)))
    out_grad = bell_draw(part_splits[1], (TOKENS, D), 1.0, 6.0, ((0, 4), (1, 4)))
    experts_keys = jax.random.split(jax.random.fold_in(part_splits[2], 1), TOKENS // TOK_DEV)
    experts_turns = jax.random.permutation(jax.random.fold_in(part_splits[2], 3), TOKENS // TOK_DEV)
    experts = jax.vmap(lambda own, number: assign_block(jax.random.fold_in(part_splits[2], 2), own, number, TOK_DEV, EXPERTS, 2, SLOT, 2))(experts_keys, experts_turns).reshape((TOKENS, 2))
    route_gates = jnp.clip(0.1 + 0.79999997 * jax.random.uniform(part_splits[3], (TOKENS, 2), jnp.float32) ** steps_of(part_splits[3], (TOKENS, 2), ((0, 4),), -0.2, 0.2), 0.1, 0.9)
    gate_proj = bell_draw(key_of[4], (EXPERTS, D, FF), D ** -0.5, 0.109375, ((0, 4), (2, 4)))
    up_proj = bell_draw(key_of[5], (EXPERTS, D, FF), D ** -0.5, 0.109375, ((0, 4), (2, 4)))
    down_proj = bell_draw(key_of[6], (EXPERTS, FF, D), FF ** -0.5, 0.0625, ((0, 4), (1, 4)))
    gate_in = bell_draw(key_of[7], (EXPERTS, RANK, D), D ** -0.5, 0.109375, ((0, 4), (2, 4)))
    gate_out = bell_draw(key_of[8], (EXPERTS, RANK, FF), 0.1, 0.59765625, ((0, 4), (2, 4)))
    up_in = bell_draw(key_of[9], (EXPERTS, RANK, D), D ** -0.5, 0.109375, ((0, 4), (2, 4)))
    up_out = bell_draw(key_of[10], (EXPERTS, RANK, FF), 0.1, 0.59765625, ((0, 4), (2, 4)))
    down_in = bell_draw(key_of[11], (EXPERTS, RANK, FF), FF ** -0.5, 0.0625, ((0, 4), (2, 4)))
    down_out = bell_draw(key_of[12], (EXPERTS, RANK, D), 0.1, 0.59765625, ((0, 4), (2, 4)))
    return {"inputs": inputs, "out_grad": out_grad, "experts": experts, "route_gates": route_gates, "gate_proj": gate_proj, "up_proj": up_proj, "down_proj": down_proj, "gate_in": gate_in, "gate_out": gate_out, "up_in": up_in, "up_out": up_out, "down_in": down_in, "down_out": down_out}


adapter_scale = 0.25


def reference(inputs, out_grad, experts, route_gates, gate_proj, up_proj, down_proj, gate_in, gate_out, up_in, up_out, down_in, down_out):
    group_total = N_EXPERT
    flat_exp = experts.reshape(group_total, 2 * TOK_DEV)
    onehot = (flat_exp[:, :, None] == jnp.arange(EXPERTS, dtype=jnp.int32)[None, None, :]).astype(jnp.int32)
    earlier = jnp.sum((jnp.cumsum(onehot, axis=1) - 1) * onehot, axis=2)
    column = (jnp.arange(group_total, dtype=jnp.int32)[:, None] * SLOT + earlier).reshape(-1)
    pair_ids = jnp.arange(2 * TOKENS, dtype=jnp.int32)
    table = jnp.full((EXPERTS, group_total * SLOT), -1, jnp.int32).at[flat_exp.reshape(-1), column].set(pair_ids)
    scaled = (route_gates[:, :, None] * out_grad[:, None, :].astype(jnp.float32)).astype(jnp.bfloat16).reshape(2 * TOKENS, D)
    block_width = FF // N_CUTS

    def per_expert(data):
        slot_ids, gate_weight, up_weight, down_weight, gin, gate_output_rows, uin, up_output_rows, down_input_grad, dout = data
        occupied = slot_ids >= 0
        safe_ids = jnp.maximum(slot_ids, 0)
        input_row_block = jnp.where(occupied[:, None], inputs[safe_ids // 2], jnp.zeros((), jnp.bfloat16))
        gradient_row_block = jnp.where(occupied[:, None], scaled[safe_ids], jnp.zeros((), jnp.bfloat16))
        gate_low_rank = jnp.dot(input_row_block, gin.T, preferred_element_type=jnp.float32).astype(jnp.bfloat16)
        up_low_rank = jnp.dot(input_row_block, uin.T, preferred_element_type=jnp.float32).astype(jnp.bfloat16)
        gate_preactivation = jnp.dot(input_row_block, gate_weight, preferred_element_type=jnp.float32) + adapter_scale * jnp.dot(gate_low_rank, gate_output_rows, preferred_element_type=jnp.float32)
        up_preactivation = jnp.dot(input_row_block, up_weight, preferred_element_type=jnp.float32) + adapter_scale * jnp.dot(up_low_rank, up_output_rows, preferred_element_type=jnp.float32)
        sigmoid_gate = jax.nn.sigmoid(gate_preactivation)
        activated = gate_preactivation * sigmoid_gate
        hidden_state = (activated * up_preactivation).astype(jnp.bfloat16)
        down_low_rank = jnp.dot(gradient_row_block, dout.T, preferred_element_type=jnp.float32).astype(jnp.bfloat16)
        hidden_state_gradient = jnp.dot(gradient_row_block, down_weight.T, preferred_element_type=jnp.float32) + adapter_scale * jnp.dot(down_low_rank, down_input_grad, preferred_element_type=jnp.float32)
        gate_preact_grad = (hidden_state_gradient * up_preactivation * sigmoid_gate * (1.0 + gate_preactivation * (1.0 - sigmoid_gate))).astype(jnp.bfloat16)
        up_preact_grad = (hidden_state_gradient * activated).astype(jnp.bfloat16)
        gate_projected = jnp.dot(gate_preact_grad, gate_output_rows.T, preferred_element_type=jnp.float32)
        up_projected = jnp.dot(up_preact_grad, up_output_rows.T, preferred_element_type=jnp.float32)
        down_projected = jnp.dot(hidden_state, down_input_grad.T, preferred_element_type=jnp.float32)
        gradient_gate_output = adapter_scale * jnp.dot(gate_low_rank.T, gate_preact_grad, preferred_element_type=jnp.float32)
        gradient_up_output = adapter_scale * jnp.dot(up_low_rank.T, up_preact_grad, preferred_element_type=jnp.float32)
        gradient_down_input = adapter_scale * jnp.dot(down_low_rank.T, hidden_state, preferred_element_type=jnp.float32)
        widened_input = input_row_block.astype(jnp.float32)
        gradient_gate_input = adapter_scale * jnp.dot(gate_projected.T, widened_input, precision=lax.Precision.HIGHEST)
        gradient_up_input = adapter_scale * jnp.dot(up_projected.T, widened_input, precision=lax.Precision.HIGHEST)
        gradient_down_output = adapter_scale * jnp.dot(down_projected.T, gradient_row_block.astype(jnp.float32), precision=lax.Precision.HIGHEST)
        gate_input_wide = gin.astype(jnp.float32)
        up_input_wide = uin.astype(jnp.float32)
        row_count = input_row_block.shape[0]

        def split_units(array):
            return jnp.swapaxes(array.reshape(array.shape[0], N_CUTS, block_width), 0, 1)

        blocks = (split_units(gate_preact_grad), split_units(up_preact_grad), split_units(gate_weight), split_units(up_weight), split_units(gate_output_rows), split_units(up_output_rows))

        def add_block(running, block_data):
            gate_part, up_part, wgate_part, wup_part, gout_part, uout_part = block_data
            gate_partial = jnp.dot(gate_part, gout_part.T, preferred_element_type=jnp.float32)
            up_partial = jnp.dot(up_part, uout_part.T, preferred_element_type=jnp.float32)
            partial_product = jnp.dot(gate_part, wgate_part.T, preferred_element_type=jnp.float32) + jnp.dot(up_part, wup_part.T, preferred_element_type=jnp.float32)
            partial_product = partial_product + adapter_scale * (jnp.dot(gate_partial, gate_input_wide, precision=lax.Precision.HIGHEST) + jnp.dot(up_partial, up_input_wide, precision=lax.Precision.HIGHEST))
            rounded = lax.optimization_barrier(partial_product.astype(jnp.bfloat16))
            return running + rounded.astype(jnp.float32), None

        running, unused = lax.scan(add_block, jnp.zeros((row_count, D), jnp.float32), blocks)
        row_grad = running.astype(jnp.bfloat16)
        return row_grad, gradient_gate_input, gradient_gate_output, gradient_up_input, gradient_up_output, gradient_down_input, gradient_down_output

    results = lax.map(per_expert, (table, gate_proj, up_proj, down_proj, gate_in, gate_out, up_in, up_out, down_in, down_out))
    row_grads, grad_gate_in, gate_output_gradient, grad_up_in, up_output_gradient, down_input_gradient, grad_down_out = results
    flat_table = table.reshape(-1)
    occupied_all = flat_table >= 0
    landing = jnp.zeros((2 * TOKENS, D), jnp.float32).at[jnp.maximum(flat_table, 0)].add(
        jnp.where(occupied_all[:, None], row_grads.reshape(-1, D).astype(jnp.float32), 0.0))
    input_grad = jnp.sum(landing.reshape(TOKENS, 2, D), axis=1).astype(jnp.bfloat16)
    return (input_grad, grad_gate_in, gate_output_gradient, grad_up_in, up_output_gradient, down_input_gradient, grad_down_out)
```

```python
import functools

import jax
import jax.numpy as jnp
from jax import lax
from jax.experimental import pallas as pl
from jax.experimental.pallas import tpu as pltpu
from jax.sharding import PartitionSpec as P

EXPERTS = 8
SLOT = 64

adapter_scale = 0.25

F32 = jnp.float32
BF16 = jnp.bfloat16
NN = (((1,), (0,)), ((), ()))
NT = (((1,), (1,)), ((), ()))


def mm(a, b, dims=NN):
    return lax.dot_general(a, b, dims, preferred_element_type=F32)


def params(semantics):
    return pltpu.CompilerParams(dimension_semantics=semantics, vmem_limit_bytes=56 * 1024 * 1024)


def swap(x, k, axis):
    n = lax.axis_size(axis)
    return lax.ppermute(x, axis, [(i, i ^ k) for i in range(n)])


def forward_kernel(x_ref, wg_ref, wu_ref, low_ref, go_ref, uo_ref, a_ref, b_ref, h_ref):
    x = x_ref[0]
    rank = go_ref.shape[1]
    low = low_ref[0]
    gate = mm(x, wg_ref[0]) + adapter_scale * mm(low[:, :rank], go_ref[0])
    up = mm(x, wu_ref[0]) + adapter_scale * mm(low[:, rank:], uo_ref[0])
    q = jax.nn.sigmoid(gate)
    silu = gate * q
    a_ref[0] = (up * q * (1.0 + gate * (1.0 - q))).astype(BF16)
    b_ref[0] = silu.astype(BF16)
    h_ref[0] = (silu * up).astype(BF16)


def forward(rows, wg, wu, low, go, uo):
    count, n, width = rows.shape
    units = wg.shape[2]
    rank = go.shape[1]
    ft = min(512, units)
    out = jax.ShapeDtypeStruct((count, n, units), BF16)
    wide = pl.BlockSpec((1, n, ft), lambda l, f: (l, 0, f))
    weight = pl.BlockSpec((1, width, ft), lambda l, f: (l, 0, f))
    factor = pl.BlockSpec((1, rank, ft), lambda l, f: (l, 0, f))
    return pl.pallas_call(
        forward_kernel,
        grid=(count, units // ft),
        in_specs=[
            pl.BlockSpec((1, n, width), lambda l, f: (l, 0, 0)),
            weight,
            weight,
            pl.BlockSpec((1, n, 2 * rank), lambda l, f: (l, 0, 0)),
            factor,
            factor,
        ],
        out_specs=[wide, wide, wide],
        out_shape=[out, out, out],
        compiler_params=params(("arbitrary", "arbitrary")),
        cost_estimate=pl.CostEstimate(
            flops=4 * count * n * width * units,
            bytes_accessed=4 * count * width * units,
            transcendentals=count * n * units,
        ),
        name="forward_units",
    )(rows, wg, wu, low, go, uo)


def hidden_kernel(
    g_ref, wd_ref, low_ref, lowt_ref, di_ref, go_ref, uo_ref, a_ref, b_ref, h_ref,
    gg_ref, ug_ref, ggo_ref, guo_ref, gdi_ref, proj_ref,
):
    rank = di_ref.shape[1]
    hg = mm(g_ref[0], wd_ref[0], NT) + adapter_scale * mm(low_ref[0], di_ref[0])
    gg = (hg * a_ref[0].astype(F32)).astype(BF16)
    ug = (hg * b_ref[0].astype(F32)).astype(BF16)
    h = h_ref[0]
    gg_ref[0] = gg
    ug_ref[0] = ug
    lowt = lowt_ref[0]
    ggo_ref[0] = adapter_scale * mm(lowt[:rank], gg)
    guo_ref[0] = adapter_scale * mm(lowt[rank : 2 * rank], ug)
    gdi_ref[0] = adapter_scale * mm(lowt[2 * rank :], h)
    proj = jnp.concatenate(
        [mm(gg, go_ref[0], NT), mm(ug, uo_ref[0], NT), mm(h, di_ref[0], NT)], axis=1
    )

    @pl.when(pl.program_id(1) == 0)
    def _():
        proj_ref[0] = proj

    @pl.when(pl.program_id(1) > 0)
    def _():
        proj_ref[0] = proj_ref[0] + proj


def hidden_back(rows, wd, low, lowt, di, go, uo, a, b, h):
    count, n, width = rows.shape
    units = wd.shape[1]
    rank = di.shape[1]
    ft = min(512, units)
    wide = pl.BlockSpec((1, n, ft), lambda l, f: (l, 0, f))
    factor = pl.BlockSpec((1, rank, ft), lambda l, f: (l, 0, f))
    return pl.pallas_call(
        hidden_kernel,
        grid=(count, units // ft),
        in_specs=[
            pl.BlockSpec((1, n, width), lambda l, f: (l, 0, 0)),
            pl.BlockSpec((1, ft, width), lambda l, f: (l, f, 0)),
            pl.BlockSpec((1, n, rank), lambda l, f: (l, 0, 0)),
            pl.BlockSpec((1, 3 * rank, n), lambda l, f: (l, 0, 0)),
            factor,
            factor,
            factor,
            wide,
            wide,
            wide,
        ],
        out_specs=[
            wide,
            wide,
            factor,
            factor,
            factor,
            pl.BlockSpec((1, n, 3 * rank), lambda l, f: (l, 0, 0)),
        ],
        out_shape=[
            jax.ShapeDtypeStruct((count, n, units), BF16),
            jax.ShapeDtypeStruct((count, n, units), BF16),
            jax.ShapeDtypeStruct((count, rank, units), F32),
            jax.ShapeDtypeStruct((count, rank, units), F32),
            jax.ShapeDtypeStruct((count, rank, units), F32),
            jax.ShapeDtypeStruct((count, n, 3 * rank), F32),
        ],
        compiler_params=params(("arbitrary", "arbitrary")),
        cost_estimate=pl.CostEstimate(
            flops=2 * count * n * width * units,
            bytes_accessed=2 * count * width * units,
            transcendentals=0,
        ),
        name="hidden_back",
    )(rows, wd, low, lowt, di, go, uo, a, b, h)


def rows_kernel(with_adapter, place_ref, gg_ref, ug_ref, wg_ref, wu_ref, back_ref, *rest):
    if with_adapter:
        proj_ref, in_ref, out_ref, y_ref = rest
    else:
        out_ref, y_ref = rest
    l = pl.program_id(1)
    count = pl.num_programs(1)
    y = mm(gg_ref[0], wg_ref[0], NT) + mm(ug_ref[0], wu_ref[0], NT)
    if with_adapter:
        y = y + adapter_scale * mm(proj_ref[0], in_ref[0])
    groups = back_ref.shape[0]
    tokens = back_ref.shape[1]
    y_ref[l] = y.astype(BF16).reshape(groups, SLOT, -1)

    @pl.when(l == count - 1)
    def _():
        for g in range(groups):
            held = y_ref[:, g].reshape(-1, y_ref.shape[3])
            out_ref[g * tokens : (g + 1) * tokens] = mm(back_ref[g], held).astype(BF16)


def row_back(place, gg, ug, wg, wu, back, span, adapter=None):
    count, n, units = gg.shape
    groups, tokens, _ = back.shape
    dt = 384 if span % 384 == 0 else span
    tiles = span // dt
    rows_spec = pl.BlockSpec((1, n, units), lambda d, l, p: (l, 0, 0))
    weight = pl.BlockSpec((1, dt, units), lambda d, l, p: (l, p[0] * tiles + d, 0))
    in_specs = [
        rows_spec,
        rows_spec,
        weight,
        weight,
        pl.BlockSpec(back.shape, lambda d, l, p: (0, 0, 0)),
    ]
    operands = [gg, ug, wg, wu, back]
    if adapter is not None:
        proj, factor = adapter
        in_specs += [
            pl.BlockSpec((1, n, proj.shape[2]), lambda d, l, p: (l, 0, 0)),
            pl.BlockSpec((1, factor.shape[1], dt), lambda d, l, p: (l, 0, d)),
        ]
        operands += [proj, factor]
    return pl.pallas_call(
        functools.partial(rows_kernel, adapter is not None),
        grid_spec=pltpu.PrefetchScalarGridSpec(
            num_scalar_prefetch=1,
            grid=(tiles, count),
            in_specs=in_specs,
            out_specs=pl.BlockSpec((groups * tokens, dt), lambda d, l, p: (0, d)),
            scratch_shapes=[pltpu.VMEM((count, groups, SLOT, dt), BF16)],
        ),
        out_shape=jax.ShapeDtypeStruct((groups * tokens, span), BF16),
        compiler_params=params(("arbitrary", "arbitrary")),
        cost_estimate=pl.CostEstimate(
            flops=4 * count * n * span * units,
            bytes_accessed=4 * count * span * units,
            transcendentals=0,
        ),
        name="row_back",
    )(place, *operands)


def routing(ids, gates, me, order, local_count):
    groups, tokens, _ = ids.shape
    flat = ids.reshape(groups, 2 * tokens)
    onehot = (flat[:, :, None] == jnp.arange(EXPERTS, dtype=jnp.int32)).astype(jnp.int32)
    earlier = jnp.sum((jnp.cumsum(onehot, axis=1) - 1) * onehot, axis=2)
    target = (flat * SLOT + earlier).reshape(groups, 1, tokens, 2)
    slots = me * (local_count * SLOT) + jnp.arange(local_count * SLOT, dtype=jnp.int32)
    match = target == slots[None, :, None, None]
    match = jnp.take(match, order, axis=0)
    gates = jnp.take(gates, order, axis=0)
    place = jnp.any(match, axis=3).astype(BF16)
    slot_gate = jnp.sum(jnp.where(match, gates[:, None], 0.0), axis=(2, 3))
    return place, jnp.swapaxes(place, 1, 2), slot_gate


def body(
    inputs,
    out_grad,
    experts,
    route_gates,
    gate_proj,
    up_proj,
    down_proj,
    gate_in,
    gate_out,
    up_in,
    up_out,
    down_in,
    down_out,
):
    groups = lax.axis_size("expert")
    cuts = lax.axis_size("cuts")
    me = lax.axis_index("expert")
    cut = lax.axis_index("cuts")
    count = gate_proj.shape[0]
    tokens, col = inputs.shape
    width = gate_proj.shape[1]
    rank = gate_in.shape[1]
    n = groups * SLOT
    paired = groups == 4 and cuts == 4

    routes = lax.all_gather(
        jnp.concatenate([experts.astype(F32), route_gates], axis=1), "expert"
    )
    relative = jnp.array([0, 2, 1, 3] if paired else list(range(groups)), jnp.int32)
    order = relative ^ me if paired else relative
    place, back, slot_gate = routing(
        routes[:, :, :2].astype(jnp.int32), routes[:, :, 2:], me, order, count
    )

    def to_rows(held, gate=None):
        rows = jnp.einsum("gst,gtd->gsd", place, held, preferred_element_type=F32)
        if gate is not None:
            rows = rows * gate[:, :, None]
        rows = rows.astype(BF16).reshape(groups, count, SLOT, -1)
        return jnp.swapaxes(rows, 0, 1).reshape(count, n, -1)

    def spread(x):
        if not paired:
            return lax.all_gather(x, "expert")
        mine = jnp.stack([x, swap(x, 2, "expert")])
        return jnp.concatenate([mine, swap(mine, 1, "expert")])

    def sum_cuts(x):
        if not paired:
            return lax.psum(x, "cuts")
        x = x.astype(BF16)
        total = x.astype(F32)
        for k in (1, 2, 3):
            total = total + swap(x, k, "cuts").astype(F32)
        return total

    def collect(x, gate=None):
        if not paired:
            own = to_rows(spread(x), gate)
            return lax.all_gather(own, "cuts", axis=2, tiled=True), own
        arrived = [x] + [swap(x, k, "cuts") for k in (1, 2, 3)]
        rows = jnp.zeros((count, n, width), BF16)
        own = None
        for k in range(4):
            part = to_rows(spread(arrived[k]), gate)
            if k == 0:
                own = part
            rows = lax.dynamic_update_slice(rows, part, (0, 0, (cut ^ k) * col))
        return rows, own

    rows_x, own_x = collect(inputs)
    factor_x = jnp.concatenate([gate_in, up_in], axis=1)
    low_x = sum_cuts(
        jnp.einsum("lnd,lrd->lnr", own_x, factor_x, preferred_element_type=F32)
    ).astype(BF16)
    a, b, h = forward(rows_x, gate_proj, up_proj, low_x, gate_out, up_out)

    rows_g, own_g = collect(out_grad, slot_gate)
    low_g = sum_cuts(
        jnp.einsum("lnd,lrd->lnr", own_g, down_out, preferred_element_type=F32)
    ).astype(BF16)
    lowt = jnp.swapaxes(jnp.concatenate([low_x, low_g], axis=2), 1, 2)
    gg, ug, gate_output_gradient, up_output_gradient, down_input_gradient, proj = hidden_back(
        rows_g, down_proj, low_g, lowt, down_in, gate_out, up_out, a, b, h
    )
    proj = sum_cuts(proj).astype(BF16)
    proj_x = proj[:, :, : 2 * rank]
    proj_g = proj[:, :, 2 * rank :]
    grad_x = adapter_scale * jnp.einsum(
        "lnr,lnd->lrd", proj_x, own_x, preferred_element_type=F32
    )
    grad_down_out = adapter_scale * jnp.einsum(
        "lnr,lnd->lrd", proj_g, own_g, preferred_element_type=F32
    )

    back_rows = functools.partial(row_back, gg=gg, ug=ug, wg=gate_proj, wu=up_proj, back=back)
    if paired:
        total = jnp.zeros((tokens, col), F32)
        for k in (2, 3, 1, 0):
            chunk = back_rows(
                jnp.reshape(cut ^ k, (1,)).astype(jnp.int32),
                span=col,
                adapter=(proj_x, factor_x) if k == 0 else None,
            )
            half = 2 * tokens
            chunk = chunk[:half].astype(F32) + swap(chunk[half:], 1, "expert").astype(F32)
            chunk = chunk[:tokens] + swap(chunk[tokens:].astype(BF16), 2, "expert").astype(F32)
            if k:
                chunk = swap(chunk.astype(BF16), k, "cuts").astype(F32)
            total = total + chunk
        input_grad = total.astype(BF16)
    else:
        chunk = back_rows(jnp.zeros((1,), jnp.int32), span=width)
        local = mm_adapter(proj_x, factor_x, back)
        chunk = chunk.astype(F32) + lax.dynamic_update_slice(
            jnp.zeros(chunk.shape, F32), local, (0, cut * col)
        )
        chunk = lax.psum_scatter(
            chunk.astype(BF16), "expert", scatter_dimension=0, tiled=True
        )
        input_grad = lax.psum_scatter(chunk, "cuts", scatter_dimension=1, tiled=True)
    return (
        input_grad,
        grad_x[:, :rank],
        gate_output_gradient,
        grad_x[:, rank:],
        up_output_gradient,
        down_input_gradient,
        grad_down_out,
    )


def mm_adapter(proj, factor, back):
    count, n, _ = proj.shape
    groups, tokens, _ = back.shape
    term = adapter_scale * jnp.einsum("lnr,lrd->lnd", proj, factor, preferred_element_type=F32)
    term = term.astype(BF16).reshape(count, groups, SLOT, -1)
    term = jnp.swapaxes(term, 0, 1).reshape(groups, count * SLOT, -1)
    return jnp.einsum("gts,gsd->gtd", back, term, preferred_element_type=F32).reshape(
        groups * tokens, -1
    )


def solution(mesh):
    return jax.shard_map(
        body,
        mesh=mesh,
        in_specs=(
            P(("parts", "expert"), "cuts"),
            P(("parts", "expert"), "cuts"),
            P(("parts", "expert"), None),
            P(("parts", "expert"), None),
            P("expert", None, "cuts"),
            P("expert", None, "cuts"),
            P("expert", "cuts", None),
            P("expert", None, "cuts"),
            P("expert", None, "cuts"),
            P("expert", None, "cuts"),
            P("expert", None, "cuts"),
            P("expert", None, "cuts"),
            P("expert", None, "cuts"),
        ),
        out_specs=(
            P(("parts", "expert"), "cuts"),
            P(("parts", "expert"), None, "cuts"),
            P(("parts", "expert"), None, "cuts"),
            P(("parts", "expert"), None, "cuts"),
            P(("parts", "expert"), None, "cuts"),
            P(("parts", "expert"), None, "cuts"),
            P(("parts", "expert"), None, "cuts"),
        ),
        check_vma=False,
    )
```

```python
import functools

import jax
import jax.numpy as jnp
from jax import lax
from jax.experimental import pallas as pl
from jax.experimental.pallas import tpu as pltpu
from jax.sharding import PartitionSpec as P

EXPERTS = 8
SLOT = 64

adapter_scale = 0.25

F32 = jnp.float32
BF16 = jnp.bfloat16
NN = (((1,), (0,)), ((), ()))
NT = (((1,), (1,)), ((), ()))


def mm(a, b, dims=NN):
    return lax.dot_general(a, b, dims, preferred_element_type=F32)


def params(semantics):
    return pltpu.CompilerParams(dimension_semantics=semantics, vmem_limit_bytes=56 * 1024 * 1024)


def swap(x, k, axis):
    n = lax.axis_size(axis)
    return lax.ppermute(x, axis, [(i, i ^ k) for i in range(n)])


def without(kernel, start, number):
    def run(*refs):
        kernel(*refs[:start], *refs[start + number :])

    return run


ANY = pl.BlockSpec(memory_space=pl.ANY)
COST = pl.CostEstimate(flops=1, bytes_accessed=1, transcendentals=0)


def tie(x, *others):
    return pl.pallas_call(
        lambda *refs: None,
        in_specs=[ANY] * (1 + len(others)),
        out_specs=ANY,
        out_shape=jax.ShapeDtypeStruct(x.shape, x.dtype),
        input_output_aliases={0: 0},
        cost_estimate=COST,
        name="tie",
    )(x, *others)


def place_kernel(scaled, far, at_ref, place_ref, *rest):
    if scaled:
        gate_ref, rest = rest[0], rest[1:]
    pieces, out_ref = rest[:-1], rest[-1]
    count = out_ref.shape[0]
    col = pieces[0].shape[2]
    groups = place_ref.shape[0]
    for i, k in enumerate(far):
        start = pl.multiple_of((at_ref[0] ^ k) * col, col)
        for r in range(groups):
            rows = mm(place_ref[r], pieces[i * groups + r][0])
            if scaled:
                rows = rows * gate_ref[r]
            rows = rows.astype(BF16).reshape(count, SLOT, col)
            out_ref[:, r * SLOT : (r + 1) * SLOT, pl.ds(start, col)] = rows


def place_rows(at, place, pieces, far, count, gate=None):
    groups, slots, tokens = place.shape
    n = groups * SLOT
    col = pieces[0][0].shape[2]
    whole = lambda *shape: pl.BlockSpec(shape, lambda i, p: (0,) * len(shape))
    gates = [] if gate is None else [gate]
    return pl.pallas_call(
        functools.partial(place_kernel, gate is not None, far),
        grid_spec=pltpu.PrefetchScalarGridSpec(
            num_scalar_prefetch=1,
            grid=(1,),
            in_specs=[whole(groups, slots, tokens)]
            + [whole(groups, slots, 1) for _ in gates]
            + [
                pl.BlockSpec((1, tokens, col), lambda i, p, index=index: (index, 0, 0))
                for _, index in pieces
            ],
            out_specs=whole(count, n, len(far) * col),
        ),
        out_shape=jax.ShapeDtypeStruct((count, n, len(far) * col), BF16),
        compiler_params=params(("arbitrary",)),
        cost_estimate=COST,
        name="place_rows",
    )(at, place, *gates, *[array for array, _ in pieces])


def forward_kernel(x_ref, wg_ref, wu_ref, in_ref, go_ref, uo_ref, a_ref, b_ref, h_ref, low_ref):
    x = x_ref[0]
    rank = go_ref.shape[1]

    @pl.when(pl.program_id(1) == 0)
    def _():
        low_ref[0] = mm(x, in_ref[0], NT).astype(BF16)

    low = low_ref[0]
    gate = mm(x, wg_ref[0]) + adapter_scale * mm(low[:, :rank], go_ref[0])
    up = mm(x, wu_ref[0]) + adapter_scale * mm(low[:, rank:], uo_ref[0])
    q = jax.nn.sigmoid(gate)
    silu = gate * q
    a_ref[0] = (up * (q + silu * (1.0 - q))).astype(BF16)
    b_ref[0] = silu.astype(BF16)
    h_ref[0] = (silu * up).astype(BF16)


def forward(first, number, rows, wg, wu, factor_in, go, uo, held=()):
    count, n, width = rows.shape
    units = wg.shape[2]
    rank = go.shape[1]
    ft = min(512, units)
    out = jax.ShapeDtypeStruct((count, n, units), BF16)
    wide = pl.BlockSpec((1, n, ft), lambda l, f: (l + first, 0, f))
    weight = pl.BlockSpec((1, width, ft), lambda l, f: (l + first, 0, f))
    factor = pl.BlockSpec((1, rank, ft), lambda l, f: (l + first, 0, f))
    one = lambda *shape: pl.BlockSpec((1,) + shape, lambda l, f: (l + first, 0, 0))
    return pl.pallas_call(
        without(forward_kernel, 6, len(held)),
        grid=(number, units // ft),
        in_specs=[one(n, width), weight, weight, one(2 * rank, width), factor, factor]
        + [ANY for _ in held],
        out_specs=[wide, wide, wide, one(n, 2 * rank)],
        out_shape=[out, out, out, jax.ShapeDtypeStruct((count, n, 2 * rank), BF16)],
        input_output_aliases={6 + i: i for i in range(len(held))},
        compiler_params=params(("arbitrary", "arbitrary")),
        cost_estimate=COST,
        name="forward_units",
    )(rows, wg, wu, factor_in, go, uo, *held)


def hidden_kernel(
    g_ref, wd_ref, out_ref, di_ref, go_ref, uo_ref, a_ref, b_ref, h_ref,
    gg_ref, ug_ref, proj_ref, low_ref, sum_ref,
):
    g = g_ref[0]
    first = pl.program_id(1) == 0

    @pl.when(first)
    def _():
        low_ref[0] = mm(g, out_ref[0], NT).astype(BF16)

    hg = mm(g, wd_ref[0], NT) + adapter_scale * mm(low_ref[0], di_ref[0])
    gg = (hg * a_ref[0].astype(F32)).astype(BF16)
    ug = (hg * b_ref[0].astype(F32)).astype(BF16)
    gg_ref[0] = gg
    ug_ref[0] = ug
    proj = jnp.concatenate(
        [mm(gg, go_ref[0], NT), mm(ug, uo_ref[0], NT), mm(h_ref[0], di_ref[0], NT)], axis=1
    )
    total = jnp.where(first, 0.0, sum_ref[...]) + proj
    sum_ref[...] = total
    proj_ref[0] = total.astype(BF16)


def hidden_back(rows, wd, factor_out, di, go, uo, a, b, h):
    count, n, width = rows.shape
    units = wd.shape[1]
    rank = di.shape[1]
    ft = min(1024, units)
    wide = pl.BlockSpec((1, n, ft), lambda l, f: (l, 0, f))
    factor = pl.BlockSpec((1, rank, ft), lambda l, f: (l, 0, f))
    one = lambda *shape: pl.BlockSpec((1,) + shape, lambda l, f: (l, 0, 0))
    out = jax.ShapeDtypeStruct((count, n, units), BF16)
    return pl.pallas_call(
        hidden_kernel,
        grid=(count, units // ft),
        in_specs=[
            one(n, width),
            pl.BlockSpec((1, ft, width), lambda l, f: (l, f, 0)),
            one(rank, width),
            factor,
            factor,
            factor,
            wide,
            wide,
            wide,
        ],
        out_specs=[wide, wide, one(n, 3 * rank), one(n, rank)],
        out_shape=[
            out,
            out,
            jax.ShapeDtypeStruct((count, n, 3 * rank), BF16),
            jax.ShapeDtypeStruct((count, n, rank), BF16),
        ],
        scratch_shapes=[pltpu.VMEM((n, 3 * rank), F32)],
        compiler_params=params(("arbitrary", "arbitrary")),
        cost_estimate=COST,
        name="hidden_back",
    )(rows, wd, factor_out, di, go, uo, a, b, h)


def adapter_kernel(lowt_ref, gg_ref, ug_ref, h_ref, ggo_ref, guo_ref, gdi_ref):
    rank = ggo_ref.shape[1]
    lowt = lowt_ref[0]
    ggo_ref[0] = adapter_scale * mm(lowt[:rank], gg_ref[0])
    guo_ref[0] = adapter_scale * mm(lowt[rank : 2 * rank], ug_ref[0])
    gdi_ref[0] = adapter_scale * mm(lowt[2 * rank :], h_ref[0])


def adapter_back(lowt, gg, ug, h, wait=()):
    count, n, units = gg.shape
    rank = lowt.shape[1] // 3
    one = lambda *shape: pl.BlockSpec((1,) + shape, lambda l: (l, 0, 0))
    return pl.pallas_call(
        without(adapter_kernel, 4, len(wait)),
        grid=(count,),
        in_specs=[one(3 * rank, n)] + [one(n, units)] * 3 + [ANY for _ in wait],
        out_specs=[one(rank, units)] * 3,
        out_shape=[jax.ShapeDtypeStruct((count, rank, units), F32)] * 3,
        compiler_params=params(("arbitrary",)),
        cost_estimate=COST,
        name="adapter_back",
    )(lowt, gg, ug, h, *wait)


def rows_kernel(at_ref, gg_ref, ug_ref, wg_ref, wu_ref, back_ref, proj_ref, in_ref, *rest):
    *out_refs, y_ref = rest
    d = pl.program_id(0)
    l = pl.program_id(1)
    tiles = len(out_refs) // 2
    count = pl.num_programs(1)
    rank2 = in_ref.shape[1]
    y = mm(gg_ref[l], wg_ref[0], NT) + mm(ug_ref[l], wu_ref[0], NT)
    y = y + adapter_scale * mm(proj_ref[l][:, :rank2], in_ref[0])
    groups, tokens, _ = back_ref.shape
    y_ref[l] = y.astype(BF16).reshape(groups, SLOT, -1)

    def finish(keep_ref, send_ref):
        for g in range(groups):
            held = y_ref[:, g].reshape(-1, y_ref.shape[3])
            out_ref, at = (keep_ref, g) if g < groups // 2 else (send_ref, g - groups // 2)
            out_ref[at * tokens : (at + 1) * tokens] = mm(back_ref[g], held).astype(BF16)

    for i in range(tiles):
        pl.when((l == count - 1) & (d == i))(
            functools.partial(finish, out_refs[2 * i], out_refs[2 * i + 1])
        )


def row_back(at, gg, ug, wg, wu, back, proj, factor_in, dt, wait=()):
    count, n, units = gg.shape
    groups, tokens, _ = back.shape
    tiles = at.shape[0]
    whole = lambda *shape: pl.BlockSpec(shape, lambda d, l, p: (0,) * len(shape))
    weight = pl.BlockSpec((1, dt, units), lambda d, l, p: (l, p[d], 0))
    half = groups // 2 * tokens
    return pl.pallas_call(
        without(rows_kernel, 8, len(wait)),
        grid_spec=pltpu.PrefetchScalarGridSpec(
            num_scalar_prefetch=1,
            grid=(tiles, count),
            in_specs=[
                whole(*gg.shape),
                whole(*gg.shape),
                weight,
                weight,
                whole(*back.shape),
                whole(*proj.shape),
                pl.BlockSpec((1, factor_in.shape[1], dt), lambda d, l, p: (l, 0, p[d])),
            ]
            + [ANY for _ in wait],
            out_specs=[whole(half, dt)] * (2 * tiles),
            scratch_shapes=[pltpu.VMEM((count, groups, SLOT, dt), BF16)],
        ),
        out_shape=[jax.ShapeDtypeStruct((half, dt), BF16)] * (2 * tiles),
        compiler_params=params(("arbitrary", "arbitrary")),
        cost_estimate=COST,
        name="row_back",
    )(at, gg, ug, wg, wu, back, proj, factor_in, *wait)


def slots_of(experts):
    tokens = experts.shape[0]
    flat = experts.reshape(2 * tokens)
    onehot = (flat[:, None] == jnp.arange(EXPERTS, dtype=jnp.int32)).astype(BF16)
    pairs = jnp.arange(2 * tokens, dtype=jnp.int32)
    before = (pairs[:, None] > pairs[None, :]).astype(BF16)
    earlier = jnp.sum(mm(before, onehot) * onehot.astype(F32), axis=1)
    return (flat.astype(F32) * SLOT + earlier).reshape(tokens, 2)


def written(experts, routes, gates, col):
    tokens = experts.shape[0]
    number = experts.astype(F32)
    terms = [number, routes[:, :2] - number * SLOT]
    left = gates
    for _ in range(3):
        term = lax.reduce_precision(left, 8, 7)
        terms.append(term)
        left = left - term
    flat = jnp.concatenate(terms, axis=1).reshape(-1)
    rows = -(-flat.shape[0] // (16 * col)) * 16
    return jnp.pad(flat, (0, rows * col - flat.shape[0])).astype(BF16).reshape(rows, col)


def read(rows, tokens):
    terms = rows.reshape(-1)[: 10 * tokens].astype(F32).reshape(tokens, 10)
    gates = terms[:, 4:6] + terms[:, 6:8] + terms[:, 8:10]
    return jnp.concatenate([terms[:, :2] * SLOT + terms[:, 2:4], gates], axis=1)[None]


def routing(routes, me, count):
    slots = me * (count * SLOT) + jnp.arange(count * SLOT, dtype=jnp.int32)
    slots = slots.astype(F32)[None, :, None]
    first = routes[:, None, :, 0] == slots
    second = routes[:, None, :, 1] == slots
    gate = jnp.where(first, routes[:, None, :, 2], 0.0) + jnp.where(
        second, routes[:, None, :, 3], 0.0
    )
    place = (first | second).astype(BF16)
    slots = jnp.swapaxes(slots, 1, 2)
    back = ((routes[:, :, :1] == slots) | (routes[:, :, 1:2] == slots)).astype(BF16)
    return place, back, jnp.sum(gate, axis=2, keepdims=True)


def body(
    inputs,
    out_grad,
    experts,
    route_gates,
    gate_proj,
    up_proj,
    down_proj,
    gate_in,
    gate_out,
    up_in,
    up_out,
    down_in,
    down_out,
):
    groups = lax.axis_size("expert")
    cuts = lax.axis_size("cuts")
    me = lax.axis_index("expert")
    cut = lax.axis_index("cuts")
    count = gate_proj.shape[0]
    tokens, col = inputs.shape
    width = gate_proj.shape[1]
    rank = gate_in.shape[1]
    n = groups * SLOT
    paired = groups == 4 and cuts == 4 and count > 1
    factors = jnp.concatenate([gate_in, up_in, down_out], axis=1)
    routes = jnp.concatenate([slots_of(experts), route_gates], axis=1)

    def other_chip(x):
        return swap(x, 2, "expert")

    def other_core(x):
        return swap(x, 1, "expert")

    if paired:
        at = jnp.reshape(cut, (1,)).astype(jnp.int32)

        def over_cuts(x, k):
            return swap(x, k, "cuts")

        own = jnp.concatenate([inputs, written(experts, routes, route_gates, col)])[None]
        x2 = over_cuts(inputs[None], 2)
        own_over = other_chip(own)
        own_cross, own_both = other_core(own), other_core(own_over)
        first = [own, own_over, own_cross, own_both]
        routes = jnp.concatenate([read(x[0, tokens:], tokens) for x in first])
        place, back, gate = routing(routes, me, count)
        x13 = over_cuts(jnp.concatenate([inputs[None], x2]), 1)
        g2 = over_cuts(tie(out_grad, x2)[None], 2)
        x2_over = other_chip(x2)
        x2_cross = other_core(x2)
        x13 = tie(x13, g2, x2_over)
        g02 = jnp.concatenate([out_grad[None], g2])
        g13 = over_cuts(g02, 1)
        far_factors = over_cuts(tie(factors, x13)[None], 2)
        x13_over, x13_cross = other_chip(x13), other_core(x13)
        x13_over = tie(x13_over, g13, far_factors, x13_cross)
        x2_both, x13_both = other_core(x2_over), other_core(x13_over)
        f02 = jnp.concatenate([factors[None], far_factors])
        f13 = over_cuts(f02, 1)
        all_factors = jnp.concatenate([f02, f13])
        near = jnp.array([0, 2, 1, 3], jnp.int32)
        all_factors = jnp.take(all_factors, near[cut ^ jnp.arange(cuts)], axis=0)
        all_factors = jnp.moveaxis(all_factors, 0, 2).reshape(count, 3 * rank, width)
        at = jnp.reshape(cut, (1,)).astype(jnp.int32)
        pieces = [(x, 0) for x in first]
        pieces += [(x, 0) for x in (x2, x2_over, x2_cross, x2_both)]
        pieces += [(x, 0) for x in (x13, x13_over, x13_cross, x13_both)]
        pieces += [(x, 1) for x in (x13, x13_over, x13_cross, x13_both)]
        rows_x = place_rows(at, place, pieces, (0, 2, 1, 3), count)
    else:
        place, back, gate = routing(lax.all_gather(routes, "expert"), me, count)
        all_factors = lax.all_gather(factors, "cuts", axis=2, tiled=True)

        def collect(x, gate=None):
            x = lax.all_gather(x, "expert")
            rows = jnp.einsum("gst,gtd->gsd", place, x, preferred_element_type=F32)
            if gate is not None:
                rows = rows * gate
            rows = rows.astype(BF16).reshape(groups, count, SLOT, col)
            own = jnp.swapaxes(rows, 0, 1).reshape(count, n, col)
            return lax.all_gather(own, "cuts", axis=2, tiled=True)

        rows_x = collect(inputs)

    factors_in = all_factors[:, : 2 * rank]
    a, b, h, low_x = forward(
        0, count, rows_x, gate_proj, up_proj, factors_in, gate_out, up_out
    )
    if paired:
        pieces = []
        for x in (g02, g13):
            over, cross = other_chip(x), other_core(x)
            over = tie(over, h, cross)
            both = other_core(over)
            pieces += [(y, i) for i in range(2) for y in (x, over, cross, both)]
        rows_g = place_rows(at, place, pieces, (0, 2, 1, 3), count, gate)
    else:
        rows_g = collect(out_grad, gate)
    gg, ug, proj, low_g = hidden_back(
        rows_g, down_proj, all_factors[:, 2 * rank :], down_in, gate_out, up_out, a, b, h
    )
    lowt = jnp.swapaxes(jnp.concatenate([low_x, low_g], axis=2), 1, 2)

    if paired:
        def chunks(first, second, wait=()):
            return row_back(
                jnp.stack([cut ^ first, cut ^ second]).astype(jnp.int32),
                gg, ug, gate_proj, up_proj, back, proj, factors_in, col, wait,
            )

        def to_chip(keep, send):
            total = keep.astype(F32) + other_core(send).astype(F32)
            return total[:tokens], total[tokens:].astype(BF16)

        keep3, send3, keep1, send1 = chunks(3, 1)
        half3, send3 = to_chip(keep3, send3)
        half1, send1 = to_chip(keep1, send1)
        keep2, send2, keep0, send0 = chunks(2, 0, [send3, send1])
        over3 = tie(other_chip(send3), keep2)
        over1 = tie(other_chip(send1), keep2)
        half2, send2 = to_chip(keep2, tie(send2, over3, over1))
        half0, send0 = to_chip(keep0, send0)
        rows = proj.reshape(-1, col)
        near = swap(
            jnp.concatenate(
                [(half1 + over1.astype(F32)).astype(BF16), (half3 + over3.astype(F32)).astype(BF16), rows]
            ),
            1,
            "cuts",
        )
        grads = adapter_back(lowt, gg, ug, h, [send2, send0])
        over2 = tie(other_chip(send2), near, grads[0])
        over0 = other_chip(send0)
        near = near.astype(F32)
        rows = rows.astype(F32) + near[2 * tokens :]
        sum2 = half2 + over2.astype(F32) + near[tokens : 2 * tokens]
        far = swap(jnp.concatenate([sum2.astype(BF16), rows.astype(BF16)]), 2, "cuts").astype(F32)
        input_grad = (half0 + over0.astype(F32) + near[:tokens] + far[:tokens]).astype(BF16)
        proj = (rows + far[tokens:]).astype(BF16).reshape(proj.shape)
    else:
        grads = adapter_back(lowt, gg, ug, h)
        dt = 768 if width % 768 == 0 else width
        at = jnp.arange(width // dt, dtype=jnp.int32)
        chunks = row_back(at, gg, ug, gate_proj, up_proj, back, proj, factors_in, dt)
        partial = jnp.concatenate(
            [jnp.concatenate(chunks[i : i + 2]) for i in range(0, len(chunks), 2)], axis=1
        )
        partial = lax.psum_scatter(partial, "expert", scatter_dimension=0, tiled=True)
        input_grad = lax.psum_scatter(partial, "cuts", scatter_dimension=1, tiled=True)
        proj = lax.psum(proj.astype(F32), "cuts").astype(BF16)

    own_x = lax.dynamic_slice(rows_x, (0, 0, cut * col), (count, n, col))
    own_g = lax.dynamic_slice(rows_g, (0, 0, cut * col), (count, n, col))
    grad_x = adapter_scale * jnp.einsum(
        "lnr,lnd->lrd", proj[:, :, : 2 * rank], own_x, preferred_element_type=F32
    )
    grad_down_out = adapter_scale * jnp.einsum(
        "lnr,lnd->lrd", proj[:, :, 2 * rank :], own_g, preferred_element_type=F32
    )
    return (
        input_grad,
        grad_x[:, :rank],
        grads[0],
        grad_x[:, rank:],
        grads[1],
        grads[2],
        grad_down_out,
    )


def solution(mesh):
    return jax.shard_map(
        body,
        mesh=mesh,
        in_specs=(
            P(("parts", "expert"), "cuts"),
            P(("parts", "expert"), "cuts"),
            P(("parts", "expert"), None),
            P(("parts", "expert"), None),
            P("expert", None, "cuts"),
            P("expert", None, "cuts"),
            P("expert", "cuts", None),
            P("expert", None, "cuts"),
            P("expert", None, "cuts"),
            P("expert", None, "cuts"),
            P("expert", None, "cuts"),
            P("expert", None, "cuts"),
            P("expert", None, "cuts"),
        ),
        out_specs=(
            P(("parts", "expert"), "cuts"),
            P(("parts", "expert"), None, "cuts"),
            P(("parts", "expert"), None, "cuts"),
            P(("parts", "expert"), None, "cuts"),
            P(("parts", "expert"), None, "cuts"),
            P(("parts", "expert"), None, "cuts"),
            P(("parts", "expert"), None, "cuts"),
        ),
        check_vma=False,
    )
```

```python
import functools

import jax
import jax.numpy as jnp
from jax import lax
from jax.experimental import pallas as pl
from jax.experimental.pallas import tpu as pltpu
from jax.sharding import PartitionSpec as P

EXPERTS = 8
SLOT = 64

adapter_scale = 0.25

F32 = jnp.float32
BF16 = jnp.bfloat16
NN = (((1,), (0,)), ((), ()))
NT = (((1,), (1,)), ((), ()))
TN = (((0,), (0,)), ((), ()))


def mm(a, b, dims=NN):
    return lax.dot_general(a, b, dims, preferred_element_type=F32)


def params(semantics, mib=56):
    return pltpu.CompilerParams(dimension_semantics=semantics, vmem_limit_bytes=mib * 1024 * 1024)


def swap(x, k, axis):
    n = lax.axis_size(axis)
    return lax.ppermute(x, axis, [(i, i ^ k) for i in range(n)])


def without(kernel, start, number):
    def run(*refs):
        kernel(*refs[:start], *refs[start + number :])

    return run


ANY = pl.BlockSpec(memory_space=pl.ANY)
COST = pl.CostEstimate(flops=1, bytes_accessed=1, transcendentals=0)


def tie(x, *others):
    return pl.pallas_call(
        lambda *refs: None,
        in_specs=[ANY] * (1 + len(others)),
        out_specs=ANY,
        out_shape=jax.ShapeDtypeStruct(x.shape, x.dtype),
        input_output_aliases={0: 0},
        cost_estimate=COST,
        name="tie",
    )(x, *others)


def place_kernel(scaled, far, at_ref, place_ref, *rest):
    if scaled:
        gate_ref, rest = rest[0], rest[1:]
    pieces, out_ref = rest[:-1], rest[-1]
    count = out_ref.shape[0]
    col = pieces[0].shape[2]
    groups = place_ref.shape[0]
    for i, k in enumerate(far):
        start = pl.multiple_of((at_ref[0] ^ k) * col, col)
        for r in range(groups):
            rows = mm(place_ref[r], pieces[i * groups + r][0])
            if scaled:
                rows = rows * gate_ref[r]
            rows = rows.astype(BF16).reshape(count, SLOT, col)
            out_ref[:, r * SLOT : (r + 1) * SLOT, pl.ds(start, col)] = rows


def place_rows(at, place, pieces, far, count, gate=None):
    groups, slots, tokens = place.shape
    n = groups * SLOT
    col = pieces[0][0].shape[2]
    whole = lambda *shape: pl.BlockSpec(shape, lambda i, p: (0,) * len(shape))
    gates = [] if gate is None else [gate]
    return pl.pallas_call(
        functools.partial(place_kernel, gate is not None, far),
        grid_spec=pltpu.PrefetchScalarGridSpec(
            num_scalar_prefetch=1,
            grid=(1,),
            in_specs=[whole(groups, slots, tokens)]
            + [whole(groups, slots, 1) for _ in gates]
            + [
                pl.BlockSpec((1, tokens, col), lambda i, p, index=index: (index, 0, 0))
                for _, index in pieces
            ],
            out_specs=whole(count, n, len(far) * col),
        ),
        out_shape=jax.ShapeDtypeStruct((count, n, len(far) * col), BF16),
        compiler_params=params(("arbitrary",), 61),
        cost_estimate=COST,
        name="place_rows",
    )(at, place, *gates, *[array for array, _ in pieces])


def low_rank(rows_ref, at_ref, far, factor_refs, ranks):
    total = 0.0
    for k, ref in zip(far, factor_refs):
        col = ref.shape[3]
        columns = pl.ds(pl.multiple_of((at_ref[0] ^ k) * col, col), col) if len(far) > 1 else slice(None)
        total = total + mm(rows_ref[0, :, columns], ref[0, 0, ranks], NT)
    return total.astype(BF16)


def factor_specs(factors):
    return [
        pl.BlockSpec((1, 1) + array.shape[2:], lambda l, f, p, index=index: (index, l, 0, 0))
        for array, index in factors
    ]


def forward_kernel(far, at_ref, x_ref, wg_ref, wu_ref, go_ref, uo_ref, *rest):
    *factor_refs, a_ref, b_ref, h_ref, low_ref = rest
    x = x_ref[0]
    rank = go_ref.shape[1]

    @pl.when(pl.program_id(1) == 0)
    def _():
        low_ref[0] = low_rank(x_ref, at_ref, far, factor_refs, slice(0, 2 * rank))

    low = low_ref[0]
    units = go_ref.shape[2]
    step = min(512, units)
    for start in range(0, units, step):
        f = slice(start, start + step)
        gate = mm(x, wg_ref[0, :, f]) + adapter_scale * mm(low[:, :rank], go_ref[0, :, f])
        up = mm(x, wu_ref[0, :, f]) + adapter_scale * mm(low[:, rank:], uo_ref[0, :, f])
        q = 0.5 * jnp.tanh(0.5 * gate) + 0.5
        silu = gate * q
        a_ref[0, :, f] = (up * (q + silu * (1.0 - q))).astype(BF16)
        b_ref[0, :, f] = silu.astype(BF16)
        h_ref[0, :, f] = (silu * up).astype(BF16)


def forward(at, rows, wg, wu, go, uo, factors, far):
    count, n, width = rows.shape
    units = wg.shape[2]
    rank = go.shape[1]
    ft = min(1024, units)
    out = jax.ShapeDtypeStruct((count, n, units), BF16)
    wide = pl.BlockSpec((1, n, ft), lambda l, f, p: (l, 0, f))
    weight = pl.BlockSpec((1, width, ft), lambda l, f, p: (l, 0, f))
    factor = pl.BlockSpec((1, rank, ft), lambda l, f, p: (l, 0, f))
    one = lambda *shape: pl.BlockSpec((1,) + shape, lambda l, f, p: (l, 0, 0))
    return pl.pallas_call(
        functools.partial(forward_kernel, far),
        grid_spec=pltpu.PrefetchScalarGridSpec(
            num_scalar_prefetch=1,
            grid=(count, units // ft),
            in_specs=[one(n, width), weight, weight, factor, factor] + factor_specs(factors),
            out_specs=[wide, wide, wide, one(n, 2 * rank)],
        ),
        out_shape=[out, out, out, jax.ShapeDtypeStruct((count, n, 2 * rank), BF16)],
        compiler_params=params(("arbitrary", "arbitrary")),
        cost_estimate=COST,
        name="forward_units",
    )(at, rows, wg, wu, go, uo, *[array for array, _ in factors])


def hidden_kernel(
    far, at_ref, g_ref, wd_ref, di_ref, go_ref, uo_ref, a_ref, b_ref, h_ref, *rest
):
    *factor_refs, gg_ref, ug_ref, proj_ref, low_ref, sum_ref = rest
    rank = di_ref.shape[1]
    first = pl.program_id(1) == 0

    @pl.when(first)
    def _():
        low_ref[0] = low_rank(g_ref, at_ref, far, factor_refs, slice(2 * rank, 3 * rank))

    hg = mm(g_ref[0], wd_ref[0], NT) + adapter_scale * mm(low_ref[0], di_ref[0])
    gg = (hg * a_ref[0].astype(F32)).astype(BF16)
    ug = (hg * b_ref[0].astype(F32)).astype(BF16)
    gg_ref[0] = gg
    ug_ref[0] = ug
    proj = jnp.concatenate(
        [mm(gg, go_ref[0], NT), mm(ug, uo_ref[0], NT), mm(h_ref[0], di_ref[0], NT)], axis=1
    )
    total = jnp.where(first, 0.0, sum_ref[...]) + proj
    sum_ref[...] = total
    proj_ref[0] = total.astype(BF16)


def hidden_back(at, rows, wd, di, go, uo, a, b, h, factors, far):
    count, n, width = rows.shape
    units = wd.shape[1]
    rank = di.shape[1]
    ft = min(1024, units)
    wide = pl.BlockSpec((1, n, ft), lambda l, f, p: (l, 0, f))
    factor = pl.BlockSpec((1, rank, ft), lambda l, f, p: (l, 0, f))
    one = lambda *shape: pl.BlockSpec((1,) + shape, lambda l, f, p: (l, 0, 0))
    out = jax.ShapeDtypeStruct((count, n, units), BF16)
    return pl.pallas_call(
        functools.partial(hidden_kernel, far),
        grid_spec=pltpu.PrefetchScalarGridSpec(
            num_scalar_prefetch=1,
            grid=(count, units // ft),
            in_specs=[
                one(n, width),
                pl.BlockSpec((1, ft, width), lambda l, f, p: (l, f, 0)),
                factor,
                factor,
                factor,
                wide,
                wide,
                wide,
            ]
            + factor_specs(factors),
            out_specs=[wide, wide, one(n, 3 * rank), one(n, rank)],
            scratch_shapes=[pltpu.VMEM((n, 3 * rank), F32)],
        ),
        out_shape=[
            out,
            out,
            jax.ShapeDtypeStruct((count, n, 3 * rank), BF16),
            jax.ShapeDtypeStruct((count, n, rank), BF16),
        ],
        compiler_params=params(("arbitrary", "arbitrary")),
        cost_estimate=COST,
        name="hidden_back",
    )(at, rows, wd, di, go, uo, a, b, h, *[array for array, _ in factors])


def adapter_kernel(low_x_ref, low_g_ref, gg_ref, ug_ref, h_ref, ggo_ref, guo_ref, gdi_ref):
    rank = ggo_ref.shape[1]
    low = low_x_ref[0]
    ggo_ref[0] = adapter_scale * mm(low[:, :rank], gg_ref[0], TN)
    guo_ref[0] = adapter_scale * mm(low[:, rank:], ug_ref[0], TN)
    gdi_ref[0] = adapter_scale * mm(low_g_ref[0], h_ref[0], TN)


def adapter_back(low_x, low_g, gg, ug, h, wait=()):
    count, n, units = gg.shape
    rank = low_g.shape[2]
    one = lambda *shape: pl.BlockSpec((1,) + shape, lambda l: (l, 0, 0))
    return pl.pallas_call(
        without(adapter_kernel, 5, len(wait)),
        grid=(count,),
        in_specs=[one(n, 2 * rank), one(n, rank)] + [one(n, units)] * 3 + [ANY for _ in wait],
        out_specs=[one(rank, units)] * 3,
        out_shape=[jax.ShapeDtypeStruct((count, rank, units), F32)] * 3,
        compiler_params=params(("arbitrary",)),
        cost_estimate=COST,
        name="adapter_back",
    )(low_x, low_g, gg, ug, h, *wait)


def rows_kernel(at_ref, gg_ref, ug_ref, wg_ref, wu_ref, back_ref, proj_ref, in_ref, *rest):
    *out_refs, y_ref = rest
    d = pl.program_id(0)
    l = pl.program_id(1)
    tiles = len(out_refs) // 2
    count = pl.num_programs(1)
    rank2 = in_ref.shape[2] // 3 * 2
    y = mm(gg_ref[l], wg_ref[0], NT) + mm(ug_ref[l], wu_ref[0], NT)
    y = y + adapter_scale * mm(proj_ref[l][:, :rank2], in_ref[0, 0, :rank2])
    groups, tokens, _ = back_ref.shape
    y_ref[l] = y.astype(BF16).reshape(groups, SLOT, -1)

    def finish(keep_ref, send_ref):
        for g in range(groups):
            held = y_ref[:, g].reshape(-1, y_ref.shape[3])
            out_ref, at = (keep_ref, g) if g < groups // 2 else (send_ref, g - groups // 2)
            out_ref[at * tokens : (at + 1) * tokens] = mm(back_ref[g], held).astype(BF16)

    for i in range(tiles):
        pl.when((l == count - 1) & (d == i))(
            functools.partial(finish, out_refs[2 * i], out_refs[2 * i + 1])
        )


def row_back(at, gg, ug, wg, wu, back, proj, factors, order, dt, wait=()):
    count, n, units = gg.shape
    groups, tokens, _ = back.shape
    tiles = at.shape[0]
    whole = lambda *shape: pl.BlockSpec(shape, lambda d, l, p: (0,) * len(shape))
    weight = pl.BlockSpec((1, dt, units), lambda d, l, p: (l, p[d], 0))
    half = groups // 2 * tokens
    return pl.pallas_call(
        without(rows_kernel, 8, len(wait)),
        grid_spec=pltpu.PrefetchScalarGridSpec(
            num_scalar_prefetch=1,
            grid=(tiles, count),
            in_specs=[
                whole(*gg.shape),
                whole(*gg.shape),
                weight,
                weight,
                whole(*back.shape),
                whole(*proj.shape),
                pl.BlockSpec(
                    (1, 1, factors.shape[2], dt), lambda d, l, p: (order(d)[0], l, 0, order(d)[1])
                ),
            ]
            + [ANY for _ in wait],
            out_specs=[whole(half, dt)] * (2 * tiles),
            scratch_shapes=[pltpu.VMEM((count, groups, SLOT, dt), BF16)],
        ),
        out_shape=[jax.ShapeDtypeStruct((half, dt), BF16)] * (2 * tiles),
        compiler_params=params(("arbitrary", "arbitrary")),
        cost_estimate=COST,
        name="row_back",
    )(at, gg, ug, wg, wu, back, proj, factors, *wait)


def slots_of(experts):
    tokens = experts.shape[0]
    flat = experts.reshape(2 * tokens)
    onehot = (flat[:, None] == jnp.arange(EXPERTS, dtype=jnp.int32)).astype(BF16)
    pairs = jnp.arange(2 * tokens, dtype=jnp.int32)
    before = (pairs[:, None] > pairs[None, :]).astype(BF16)
    earlier = jnp.sum(mm(before, onehot) * onehot.astype(F32), axis=1)
    return (flat.astype(F32) * SLOT + earlier).reshape(tokens, 2)


def written(experts, routes, gates, col):
    tokens = experts.shape[0]
    number = experts.astype(F32)
    terms = [number, routes[:, :2] - number * SLOT]
    left = gates
    for _ in range(3):
        term = lax.reduce_precision(left, 8, 7)
        terms.append(term)
        left = left - term
    flat = jnp.concatenate(terms, axis=1).reshape(-1)
    rows = -(-flat.shape[0] // (16 * col)) * 16
    return jnp.pad(flat, (0, rows * col - flat.shape[0])).astype(BF16).reshape(rows, col)


def read(rows, tokens):
    terms = rows.reshape(-1)[: 10 * tokens].astype(F32).reshape(tokens, 10)
    gates = terms[:, 4:6] + terms[:, 6:8] + terms[:, 8:10]
    return jnp.concatenate([terms[:, :2] * SLOT + terms[:, 2:4], gates], axis=1)[None]


def routing(routes, me, count):
    slots = me * (count * SLOT) + jnp.arange(count * SLOT, dtype=jnp.int32)
    slots = slots.astype(F32)[None, :, None]
    first = routes[:, None, :, 0] == slots
    second = routes[:, None, :, 1] == slots
    gate = jnp.where(first, routes[:, None, :, 2], 0.0) + jnp.where(
        second, routes[:, None, :, 3], 0.0
    )
    place = (first | second).astype(BF16)
    slots = jnp.swapaxes(slots, 1, 2)
    back = ((routes[:, :, :1] == slots) | (routes[:, :, 1:2] == slots)).astype(BF16)
    return place, back, jnp.sum(gate, axis=2, keepdims=True)


def body(
    inputs,
    out_grad,
    experts,
    route_gates,
    gate_proj,
    up_proj,
    down_proj,
    gate_in,
    gate_out,
    up_in,
    up_out,
    down_in,
    down_out,
):
    groups = lax.axis_size("expert")
    cuts = lax.axis_size("cuts")
    me = lax.axis_index("expert")
    cut = lax.axis_index("cuts")
    count = gate_proj.shape[0]
    tokens, col = inputs.shape
    width = gate_proj.shape[1]
    rank = gate_in.shape[1]
    n = groups * SLOT
    paired = groups == 4 and cuts == 4 and count > 1
    factors = jnp.concatenate([gate_in, up_in, down_out], axis=1)
    routes = jnp.concatenate([slots_of(experts), route_gates], axis=1)

    def other_chip(x):
        return swap(x, 2, "expert")

    def other_core(x):
        return swap(x, 1, "expert")

    if paired:
        at = jnp.reshape(cut, (1,)).astype(jnp.int32)

        def over_cuts(x, k):
            return swap(x, k, "cuts")

        x2 = over_cuts(inputs[None], 2)
        own = jnp.concatenate([inputs, written(experts, routes, route_gates, col)])[None]
        own_over = other_chip(own)
        x2 = tie(x2, own_over)
        own_cross, own_both = other_core(own), other_core(own_over)
        x13 = over_cuts(jnp.concatenate([inputs[None], x2]), 1)
        g2 = over_cuts(tie(out_grad, x2)[None], 2)
        x2_over, x2_cross = other_chip(x2), other_core(x2)
        routes = jnp.concatenate(
            [read(x[0, tokens:], tokens) for x in (own, own_over, own_cross, own_both)]
        )
        place, back, gate = routing(routes, me, count)
        x13 = tie(x13, g2, x2_over)
        x2_both = other_core(x2_over)
        g02 = jnp.concatenate([out_grad[None], g2])
        g13 = over_cuts(g02, 1)
        far_factors = over_cuts(tie(factors, x13)[None], 2)
        x13_over, x13_cross = other_chip(x13), other_core(x13)
        x13_over = tie(x13_over, g13, far_factors, x13_cross, place, back, gate)
        x13_both = other_core(x13_over)
        f02 = jnp.concatenate([factors[None], far_factors])
        f13 = over_cuts(f02, 1)
        far = (0, 2, 1, 3)
        all_factors = [(f02, 0), (f02, 1), (f13, 0), (f13, 1)]
        at = jnp.reshape(cut, (1,)).astype(jnp.int32)
        pieces = [(x, 0) for x in (own, own_over, own_cross, own_both)]
        pieces += [(x, 0) for x in (x2, x2_over, x2_cross, x2_both)]
        pieces += [(x, 0) for x in (x13, x13_over, x13_cross, x13_both)]
        pieces += [(x, 1) for x in (x13, x13_over, x13_cross, x13_both)]
        rows_x = place_rows(at, place, pieces, far, count)
    else:
        place, back, gate = routing(lax.all_gather(routes, "expert"), me, count)
        every_factor = lax.all_gather(factors, "cuts", axis=2, tiled=True)[None]
        far, all_factors = (0,), [(every_factor, 0)]
        at = jnp.zeros((1,), jnp.int32)

        def collect(x, gate=None):
            x = lax.all_gather(x, "expert")
            rows = jnp.einsum("gst,gtd->gsd", place, x, preferred_element_type=F32)
            if gate is not None:
                rows = rows * gate
            rows = rows.astype(BF16).reshape(groups, count, SLOT, col)
            own = jnp.swapaxes(rows, 0, 1).reshape(count, n, col)
            return lax.all_gather(own, "cuts", axis=2, tiled=True)

        rows_x = collect(inputs)

    a, b, h, low_x = forward(
        at, rows_x, gate_proj, up_proj, gate_out, up_out, all_factors, far
    )
    if paired:
        pieces = []
        for x in (g02, g13):
            over, cross = other_chip(x), other_core(x)
            over = tie(over, h, cross)
            both = other_core(over)
            pieces += [(y, i) for i in range(2) for y in (x, over, cross, both)]
        rows_g = place_rows(at, place, pieces, far, count, gate)
    else:
        rows_g = collect(out_grad, gate)
    gg, ug, proj, low_g = hidden_back(
        at, rows_g, down_proj, down_in, gate_out, up_out, a, b, h, all_factors, far
    )
    own_x = lax.dynamic_slice(rows_x, (0, 0, cut * col), (count, n, col))
    own_g = lax.dynamic_slice(rows_g, (0, 0, cut * col), (count, n, col))

    def factor_grads(proj):
        grad_x = adapter_scale * jnp.einsum(
            "lnr,lnd->lrd", proj[:, :, : 2 * rank], own_x, preferred_element_type=F32
        )
        grad_g = adapter_scale * jnp.einsum(
            "lnr,lnd->lrd", proj[:, :, 2 * rank :], own_g, preferred_element_type=F32
        )
        return grad_x, grad_g

    if paired:
        def chunks(far, held, pieces, wait=()):
            return row_back(
                jnp.stack([cut ^ k for k in far]).astype(jnp.int32),
                gg, ug, gate_proj, up_proj, back, proj, held, pieces, col, wait,
            )

        def to_chip(keep, send):
            total = keep.astype(F32) + other_core(send).astype(F32)
            return total[:tokens], total[tokens:].astype(BF16)

        near_rows = swap(proj, 1, "cuts")
        keep3, send3, keep1, send1 = chunks((3, 1), f13, lambda d: (1 - d, 0))
        half3, send3 = to_chip(keep3, tie(send3, near_rows))
        half1, send1 = to_chip(keep1, tie(send1, near_rows))
        rows = proj.astype(F32) + near_rows.astype(F32)
        sent = rows.astype(BF16)
        keep2, send2 = chunks((2,), f02, lambda d: (1, 0), [send3, send1, sent])
        over3 = tie(other_chip(send3), keep2)
        over1 = tie(other_chip(send1), keep2)
        far_rows = swap(sent, 2, "cuts")
        half2, send2 = to_chip(keep2, tie(send2, over3, over1, far_rows))
        proj_all = (rows + far_rows.astype(F32)).astype(BF16)
        near = jnp.concatenate(
            [(half1 + over1.astype(F32)).astype(BF16), (half3 + over3.astype(F32)).astype(BF16)]
        )
        keep0, send0 = chunks((0,), f02, lambda d: (0, 0), [send2, near])
        near = tie(swap(near, 1, "cuts"), keep0)
        over2 = tie(other_chip(send2), keep0)
        half0, send0 = to_chip(keep0, tie(send0, near, over2))
        near = near.astype(F32)
        sum2 = (half2 + over2.astype(F32) + near[tokens:]).astype(BF16)
        grads = adapter_back(low_x, low_g, gg, ug, h, [send0, sum2])
        grad_x, grad_down_out = factor_grads(tie(proj_all, sum2))
        far = tie(swap(sum2, 2, "cuts"), grads[0], grad_x, grad_down_out).astype(F32)
        over0 = other_chip(send0).astype(F32)
        input_grad = (half0 + over0 + near[:tokens] + far).astype(BF16)
    else:
        grads = adapter_back(low_x, low_g, gg, ug, h)
        dt = 768 if width % 768 == 0 else width
        at = jnp.arange(width // dt, dtype=jnp.int32)
        chunks = row_back(
            at, gg, ug, gate_proj, up_proj, back, proj, every_factor, lambda d: (0, d), dt
        )
        partial = jnp.concatenate(
            [jnp.concatenate(chunks[i : i + 2]) for i in range(0, len(chunks), 2)], axis=1
        )
        partial = lax.psum_scatter(partial, "expert", scatter_dimension=0, tiled=True)
        input_grad = lax.psum_scatter(partial, "cuts", scatter_dimension=1, tiled=True)
        grad_x, grad_down_out = factor_grads(lax.psum(proj.astype(F32), "cuts").astype(BF16))

    return (
        input_grad,
        grad_x[:, :rank],
        grads[0],
        grad_x[:, rank:],
        grads[1],
        grads[2],
        grad_down_out,
    )


def solution(mesh):
    return jax.shard_map(
        body,
        mesh=mesh,
        in_specs=(
            P(("parts", "expert"), "cuts"),
            P(("parts", "expert"), "cuts"),
            P(("parts", "expert"), None),
            P(("parts", "expert"), None),
            P("expert", None, "cuts"),
            P("expert", None, "cuts"),
            P("expert", "cuts", None),
            P("expert", None, "cuts"),
            P("expert", None, "cuts"),
            P("expert", None, "cuts"),
            P("expert", None, "cuts"),
            P("expert", None, "cuts"),
            P("expert", None, "cuts"),
        ),
        out_specs=(
            P(("parts", "expert"), "cuts"),
            P(("parts", "expert"), None, "cuts"),
            P(("parts", "expert"), None, "cuts"),
            P(("parts", "expert"), None, "cuts"),
            P(("parts", "expert"), None, "cuts"),
            P(("parts", "expert"), None, "cuts"),
            P(("parts", "expert"), None, "cuts"),
        ),
        check_vma=False,
    )
```

```python
import functools

import jax
import jax.numpy as jnp
from jax import lax
from jax.experimental import pallas as pl
from jax.experimental.pallas import tpu as pltpu
from jax.sharding import PartitionSpec as P

EXPERTS = 8
SLOT = 64

adapter_scale = 0.25

F32 = jnp.float32
BF16 = jnp.bfloat16
NN = (((1,), (0,)), ((), ()))
NT = (((1,), (1,)), ((), ()))
TN = (((0,), (0,)), ((), ()))


def mm(a, b, dims=NN):
    return lax.dot_general(a, b, dims, preferred_element_type=F32)


def params(semantics, mib=56):
    return pltpu.CompilerParams(dimension_semantics=semantics, vmem_limit_bytes=mib * 1024 * 1024)


def swap(x, k, axis):
    n = lax.axis_size(axis)
    return lax.ppermute(x, axis, [(i, i ^ k) for i in range(n)])


def without(kernel, start, number):
    def run(*refs):
        kernel(*refs[:start], *refs[start + number :])

    return run


ANY = pl.BlockSpec(memory_space=pl.ANY)
COST = pl.CostEstimate(flops=1, bytes_accessed=1, transcendentals=0)


def tie(x, *others):
    return pl.pallas_call(
        lambda *refs: None,
        in_specs=[ANY] * (1 + len(others)),
        out_specs=ANY,
        out_shape=jax.ShapeDtypeStruct(x.shape, x.dtype),
        input_output_aliases={0: 0},
        cost_estimate=COST,
        name="tie",
    )(x, *others)


def place_kernel(scaled, far, at_ref, place_ref, *rest):
    if scaled:
        gate_ref, rest = rest[0], rest[1:]
    pieces, out_ref = rest[:-1], rest[-1]
    count = out_ref.shape[0]
    col = pieces[0].shape[2]
    groups = place_ref.shape[0]
    for i, k in enumerate(far):
        start = pl.multiple_of((at_ref[0] ^ k) * col, col)
        for r in range(groups):
            rows = mm(place_ref[r], pieces[i * groups + r][0])
            if scaled:
                rows = rows * gate_ref[r]
            rows = rows.astype(BF16).reshape(count, SLOT, col)
            out_ref[:, r * SLOT : (r + 1) * SLOT, pl.ds(start, col)] = rows


def place_rows(at, place, pieces, far, count, gate=None):
    groups, slots, tokens = place.shape
    n = groups * SLOT
    col = pieces[0][0].shape[2]
    whole = lambda *shape: pl.BlockSpec(shape, lambda i, p: (0,) * len(shape))
    gates = [] if gate is None else [gate]
    return pl.pallas_call(
        functools.partial(place_kernel, gate is not None, far),
        grid_spec=pltpu.PrefetchScalarGridSpec(
            num_scalar_prefetch=1,
            grid=(1,),
            in_specs=[whole(groups, slots, tokens)]
            + [whole(groups, slots, 1) for _ in gates]
            + [
                pl.BlockSpec((1, tokens, col), lambda i, p, index=index: (index, 0, 0))
                for _, index in pieces
            ],
            out_specs=whole(count, n, len(far) * col),
        ),
        out_shape=jax.ShapeDtypeStruct((count, n, len(far) * col), BF16),
        compiler_params=params(("arbitrary",), 61),
        cost_estimate=COST,
        name="place_rows",
    )(at, place, *gates, *[array for array, _ in pieces])


def low_rank(rows_ref, at_ref, far, factor_refs, ranks):
    total = 0.0
    for k, ref in zip(far, factor_refs):
        col = ref.shape[3]
        columns = pl.ds(pl.multiple_of((at_ref[0] ^ k) * col, col), col) if len(far) > 1 else slice(None)
        total = total + mm(rows_ref[0, :, columns], ref[0, 0, ranks], NT)
    return total.astype(BF16)


def factor_specs(factors):
    return [
        pl.BlockSpec((1, 1) + array.shape[2:], lambda l, f, p, index=index: (index, l, 0, 0))
        for array, index in factors
    ]


def forward_kernel(far, at_ref, x_ref, wg_ref, wu_ref, go_ref, uo_ref, *rest):
    *factor_refs, a_ref, b_ref, h_ref, low_ref = rest
    x = x_ref[0]
    rank = go_ref.shape[1]

    @pl.when(pl.program_id(1) == 0)
    def _():
        low_ref[0] = low_rank(x_ref, at_ref, far, factor_refs, slice(0, 2 * rank))

    low = low_ref[0]
    units = go_ref.shape[2]
    step = min(512, units)
    for start in range(0, units, step):
        f = slice(start, start + step)
        gate = mm(x, wg_ref[0, :, f]) + adapter_scale * mm(low[:, :rank], go_ref[0, :, f])
        up = mm(x, wu_ref[0, :, f]) + adapter_scale * mm(low[:, rank:], uo_ref[0, :, f])
        q = 0.5 * jnp.tanh(0.5 * gate) + 0.5
        silu = gate * q
        a_ref[0, :, f] = (up * (q + silu * (1.0 - q))).astype(BF16)
        b_ref[0, :, f] = silu.astype(BF16)
        h_ref[0, :, f] = (silu * up).astype(BF16)


def forward(at, rows, wg, wu, go, uo, factors, far):
    count, n, width = rows.shape
    units = wg.shape[2]
    rank = go.shape[1]
    ft = min(1024, units)
    out = jax.ShapeDtypeStruct((count, n, units), BF16)
    wide = pl.BlockSpec((1, n, ft), lambda l, f, p: (l, 0, f))
    weight = pl.BlockSpec((1, width, ft), lambda l, f, p: (l, 0, f))
    factor = pl.BlockSpec((1, rank, ft), lambda l, f, p: (l, 0, f))
    one = lambda *shape: pl.BlockSpec((1,) + shape, lambda l, f, p: (l, 0, 0))
    return pl.pallas_call(
        functools.partial(forward_kernel, far),
        grid_spec=pltpu.PrefetchScalarGridSpec(
            num_scalar_prefetch=1,
            grid=(count, units // ft),
            in_specs=[one(n, width), weight, weight, factor, factor] + factor_specs(factors),
            out_specs=[wide, wide, wide, one(n, 2 * rank)],
        ),
        out_shape=[out, out, out, jax.ShapeDtypeStruct((count, n, 2 * rank), BF16)],
        compiler_params=params(("arbitrary", "arbitrary")),
        cost_estimate=COST,
        name="forward_units",
    )(at, rows, wg, wu, go, uo, *[array for array, _ in factors])


def hidden_kernel(
    far, at_ref, g_ref, wd_ref, di_ref, go_ref, uo_ref, a_ref, b_ref, h_ref, *rest
):
    *factor_refs, gg_ref, ug_ref, proj_ref, low_ref, sum_ref = rest
    rank = di_ref.shape[1]
    first = pl.program_id(1) == 0

    @pl.when(first)
    def _():
        low_ref[0] = low_rank(g_ref, at_ref, far, factor_refs, slice(2 * rank, 3 * rank))

    hg = mm(g_ref[0], wd_ref[0], NT) + adapter_scale * mm(low_ref[0], di_ref[0])
    gg = (hg * a_ref[0].astype(F32)).astype(BF16)
    ug = (hg * b_ref[0].astype(F32)).astype(BF16)
    gg_ref[0] = gg
    ug_ref[0] = ug
    proj = jnp.concatenate(
        [mm(gg, go_ref[0], NT), mm(ug, uo_ref[0], NT), mm(h_ref[0], di_ref[0], NT)], axis=1
    )
    total = jnp.where(first, 0.0, sum_ref[...]) + proj
    sum_ref[...] = total
    proj_ref[0] = total.astype(BF16)


def hidden_back(at, rows, wd, di, go, uo, a, b, h, factors, far):
    count, n, width = rows.shape
    units = wd.shape[1]
    rank = di.shape[1]
    ft = min(1024, units)
    wide = pl.BlockSpec((1, n, ft), lambda l, f, p: (l, 0, f))
    factor = pl.BlockSpec((1, rank, ft), lambda l, f, p: (l, 0, f))
    one = lambda *shape: pl.BlockSpec((1,) + shape, lambda l, f, p: (l, 0, 0))
    out = jax.ShapeDtypeStruct((count, n, units), BF16)
    return pl.pallas_call(
        functools.partial(hidden_kernel, far),
        grid_spec=pltpu.PrefetchScalarGridSpec(
            num_scalar_prefetch=1,
            grid=(count, units // ft),
            in_specs=[
                one(n, width),
                pl.BlockSpec((1, ft, width), lambda l, f, p: (l, f, 0)),
                factor,
                factor,
                factor,
                wide,
                wide,
                wide,
            ]
            + factor_specs(factors),
            out_specs=[wide, wide, one(n, 3 * rank), one(n, rank)],
            scratch_shapes=[pltpu.VMEM((n, 3 * rank), F32)],
        ),
        out_shape=[
            out,
            out,
            jax.ShapeDtypeStruct((count, n, 3 * rank), BF16),
            jax.ShapeDtypeStruct((count, n, rank), BF16),
        ],
        compiler_params=params(("arbitrary", "arbitrary")),
        cost_estimate=COST,
        name="hidden_back",
    )(at, rows, wd, di, go, uo, a, b, h, *[array for array, _ in factors])


def adapter_kernel(low_x_ref, low_g_ref, gg_ref, ug_ref, h_ref, ggo_ref, guo_ref, gdi_ref):
    rank = ggo_ref.shape[1]
    low = low_x_ref[0]
    ggo_ref[0] = adapter_scale * mm(low[:, :rank], gg_ref[0], TN)
    guo_ref[0] = adapter_scale * mm(low[:, rank:], ug_ref[0], TN)
    gdi_ref[0] = adapter_scale * mm(low_g_ref[0], h_ref[0], TN)


def adapter_back(low_x, low_g, gg, ug, h, wait=()):
    count, n, units = gg.shape
    rank = low_g.shape[2]
    one = lambda *shape: pl.BlockSpec((1,) + shape, lambda l: (l, 0, 0))
    return pl.pallas_call(
        without(adapter_kernel, 5, len(wait)),
        grid=(count,),
        in_specs=[one(n, 2 * rank), one(n, rank)] + [one(n, units)] * 3 + [ANY for _ in wait],
        out_specs=[one(rank, units)] * 3,
        out_shape=[jax.ShapeDtypeStruct((count, rank, units), F32)] * 3,
        compiler_params=params(("arbitrary",)),
        cost_estimate=COST,
        name="adapter_back",
    )(low_x, low_g, gg, ug, h, *wait)


def rows_kernel(at_ref, gg_ref, ug_ref, wg_ref, wu_ref, back_ref, proj_ref, in_ref, *rest):
    *out_refs, y_ref = rest
    d = pl.program_id(0)
    l = pl.program_id(1)
    tiles = len(out_refs) // 2
    count = pl.num_programs(1)
    rank2 = in_ref.shape[2] // 3 * 2
    y = mm(gg_ref[l], wg_ref[0], NT) + mm(ug_ref[l], wu_ref[0], NT)
    y = y + adapter_scale * mm(proj_ref[l][:, :rank2], in_ref[0, 0, :rank2])
    groups, tokens, _ = back_ref.shape
    y_ref[l] = y.astype(BF16).reshape(groups, SLOT, -1)

    def finish(keep_ref, send_ref):
        for g in range(groups):
            held = y_ref[:, g].reshape(-1, y_ref.shape[3])
            out_ref, at = (keep_ref, g) if g < groups // 2 else (send_ref, g - groups // 2)
            out_ref[at * tokens : (at + 1) * tokens] = mm(back_ref[g], held).astype(BF16)

    for i in range(tiles):
        pl.when((l == count - 1) & (d == i))(
            functools.partial(finish, out_refs[2 * i], out_refs[2 * i + 1])
        )


def row_back(at, gg, ug, wg, wu, back, proj, factors, order, dt, wait=()):
    count, n, units = gg.shape
    groups, tokens, _ = back.shape
    tiles = at.shape[0]
    whole = lambda *shape: pl.BlockSpec(shape, lambda d, l, p: (0,) * len(shape))
    weight = pl.BlockSpec((1, dt, units), lambda d, l, p: (l, p[d], 0))
    half = groups // 2 * tokens
    return pl.pallas_call(
        without(rows_kernel, 8, len(wait)),
        grid_spec=pltpu.PrefetchScalarGridSpec(
            num_scalar_prefetch=1,
            grid=(tiles, count),
            in_specs=[
                whole(*gg.shape),
                whole(*gg.shape),
                weight,
                weight,
                whole(*back.shape),
                whole(*proj.shape),
                pl.BlockSpec(
                    (1, 1, factors.shape[2], dt), lambda d, l, p: (order(d)[0], l, 0, order(d)[1])
                ),
            ]
            + [ANY for _ in wait],
            out_specs=[whole(half, dt)] * (2 * tiles),
            scratch_shapes=[pltpu.VMEM((count, groups, SLOT, dt), BF16)],
        ),
        out_shape=[jax.ShapeDtypeStruct((half, dt), BF16)] * (2 * tiles),
        compiler_params=params(("arbitrary", "arbitrary")),
        cost_estimate=COST,
        name="row_back",
    )(at, gg, ug, wg, wu, back, proj, factors, *wait)


def slots_of(experts):
    tokens = experts.shape[0]
    flat = experts.reshape(2 * tokens)
    onehot = (flat[:, None] == jnp.arange(EXPERTS, dtype=jnp.int32)).astype(BF16)
    pairs = jnp.arange(2 * tokens, dtype=jnp.int32)
    before = (pairs[:, None] > pairs[None, :]).astype(BF16)
    earlier = jnp.sum(mm(before, onehot) * onehot.astype(F32), axis=1)
    return (flat.astype(F32) * SLOT + earlier).reshape(tokens, 2)


def written(experts, routes, gates, col):
    tokens = experts.shape[0]
    number = experts.astype(F32)
    terms = [number, routes[:, :2] - number * SLOT]
    left = gates
    for _ in range(3):
        term = lax.reduce_precision(left, 8, 7)
        terms.append(term)
        left = left - term
    flat = jnp.concatenate(terms, axis=1).reshape(-1)
    rows = -(-flat.shape[0] // (16 * col)) * 16
    return jnp.pad(flat, (0, rows * col - flat.shape[0])).astype(BF16).reshape(rows, col)


def read(rows, tokens):
    terms = rows.reshape(-1)[: 10 * tokens].astype(F32).reshape(tokens, 10)
    gates = terms[:, 4:6] + terms[:, 6:8] + terms[:, 8:10]
    return jnp.concatenate([terms[:, :2] * SLOT + terms[:, 2:4], gates], axis=1)[None]


def routing(routes, me, count):
    slots = me * (count * SLOT) + jnp.arange(count * SLOT, dtype=jnp.int32)
    slots = slots.astype(F32)[None, :, None]
    first = routes[:, None, :, 0] == slots
    second = routes[:, None, :, 1] == slots
    gate = jnp.where(first, routes[:, None, :, 2], 0.0) + jnp.where(
        second, routes[:, None, :, 3], 0.0
    )
    place = (first | second).astype(BF16)
    slots = jnp.swapaxes(slots, 1, 2)
    back = ((routes[:, :, :1] == slots) | (routes[:, :, 1:2] == slots)).astype(BF16)
    return place, back, jnp.sum(gate, axis=2, keepdims=True)


def body(
    inputs,
    out_grad,
    experts,
    route_gates,
    gate_proj,
    up_proj,
    down_proj,
    gate_in,
    gate_out,
    up_in,
    up_out,
    down_in,
    down_out,
):
    groups = lax.axis_size("expert")
    cuts = lax.axis_size("cuts")
    me = lax.axis_index("expert")
    cut = lax.axis_index("cuts")
    count = gate_proj.shape[0]
    tokens, col = inputs.shape
    width = gate_proj.shape[1]
    rank = gate_in.shape[1]
    n = groups * SLOT
    paired = groups == 4 and cuts == 4 and count > 1
    factors = jnp.concatenate([gate_in, up_in, down_out], axis=1)
    routes = jnp.concatenate([slots_of(experts), route_gates], axis=1)

    def other_chip(x):
        return swap(x, 2, "expert")

    def other_core(x):
        return swap(x, 1, "expert")

    if paired:
        at = jnp.reshape(cut, (1,)).astype(jnp.int32)

        def over_cuts(x, k):
            return swap(x, k, "cuts")

        x2 = over_cuts(inputs[None], 2)
        own = inputs[None]
        own_over = other_chip(own)
        x2 = tie(x2, own_over)
        own_cross, own_both = other_core(own), other_core(own_over)
        x13 = over_cuts(jnp.concatenate([inputs[None], x2]), 1)
        g2 = over_cuts(tie(out_grad, x2)[None], 2)
        x2_over, x2_cross = other_chip(x2), other_core(x2)
        routes = tie(written(experts, routes, route_gates, col), x2)
        over = other_chip(routes)
        routes = jnp.concatenate(
            [read(x, tokens) for x in (routes, over, other_core(routes), other_core(over))]
        )
        place, back, gate = routing(routes, me, count)
        x13 = tie(x13, g2, x2_over)
        x2_both = other_core(x2_over)
        g02 = jnp.concatenate([out_grad[None], g2])
        g13 = over_cuts(g02, 1)
        far_factors = over_cuts(tie(factors, x13)[None], 2)
        x13_over, x13_cross = other_chip(x13), other_core(x13)
        x13_over = tie(x13_over, g13, far_factors, x13_cross, place, back, gate)
        x13_both = other_core(x13_over)
        f02 = jnp.concatenate([factors[None], far_factors])
        f13 = over_cuts(f02, 1)
        far = (0, 2, 1, 3)
        all_factors = [(f02, 0), (f02, 1), (f13, 0), (f13, 1)]
        at = jnp.reshape(cut, (1,)).astype(jnp.int32)
        pieces = [(x, 0) for x in (own, own_over, own_cross, own_both)]
        pieces += [(x, 0) for x in (x2, x2_over, x2_cross, x2_both)]
        pieces += [(x, 0) for x in (x13, x13_over, x13_cross, x13_both)]
        pieces += [(x, 1) for x in (x13, x13_over, x13_cross, x13_both)]
        rows_x = place_rows(at, place, pieces, far, count)
    else:
        place, back, gate = routing(lax.all_gather(routes, "expert"), me, count)
        every_factor = lax.all_gather(factors, "cuts", axis=2, tiled=True)[None]
        far, all_factors = (0,), [(every_factor, 0)]
        at = jnp.zeros((1,), jnp.int32)

        def collect(x, gate=None):
            x = lax.all_gather(x, "expert")
            rows = jnp.einsum("gst,gtd->gsd", place, x, preferred_element_type=F32)
            if gate is not None:
                rows = rows * gate
            rows = rows.astype(BF16).reshape(groups, count, SLOT, col)
            own = jnp.swapaxes(rows, 0, 1).reshape(count, n, col)
            return lax.all_gather(own, "cuts", axis=2, tiled=True)

        rows_x = collect(inputs)

    a, b, h, low_x = forward(
        at, rows_x, gate_proj, up_proj, gate_out, up_out, all_factors, far
    )
    if paired:
        pieces = []
        for x in (g02, g13):
            over, cross = other_chip(x), other_core(x)
            over = tie(over, h, cross)
            both = other_core(over)
            pieces += [(y, i) for i in range(2) for y in (x, over, cross, both)]
        rows_g = place_rows(at, place, pieces, far, count, gate)
    else:
        rows_g = collect(out_grad, gate)
    gg, ug, proj, low_g = hidden_back(
        at, rows_g, down_proj, down_in, gate_out, up_out, a, b, h, all_factors, far
    )
    own_x = lax.dynamic_slice(rows_x, (0, 0, cut * col), (count, n, col))
    own_g = lax.dynamic_slice(rows_g, (0, 0, cut * col), (count, n, col))

    def factor_grads(proj):
        grad_x = adapter_scale * jnp.einsum(
            "lnr,lnd->lrd", proj[:, :, : 2 * rank], own_x, preferred_element_type=F32
        )
        grad_g = adapter_scale * jnp.einsum(
            "lnr,lnd->lrd", proj[:, :, 2 * rank :], own_g, preferred_element_type=F32
        )
        return grad_x, grad_g

    if paired:
        def chunks(far, held, pieces, wait=()):
            return row_back(
                jnp.stack([cut ^ k for k in far]).astype(jnp.int32),
                gg, ug, gate_proj, up_proj, back, proj, held, pieces, col, wait,
            )

        def to_chip(keep, send):
            total = keep.astype(F32) + other_core(send).astype(F32)
            return total[:tokens], total[tokens:].astype(BF16)

        near_rows = swap(proj, 1, "cuts")
        keep3, send3, keep1, send1 = chunks((3, 1), f13, lambda d: (1 - d, 0))
        half3, send3 = to_chip(keep3, tie(send3, near_rows))
        half1, send1 = to_chip(keep1, tie(send1, near_rows))
        rows = proj.astype(F32) + near_rows.astype(F32)
        sent = rows.astype(BF16)
        keep2, send2 = chunks((2,), f02, lambda d: (1, 0), [send3, send1, sent])
        over3 = tie(other_chip(send3), keep2)
        over1 = tie(other_chip(send1), keep2)
        far_rows = swap(sent, 2, "cuts")
        half2, send2 = to_chip(keep2, tie(send2, over3, over1, far_rows))
        proj_all = (rows + far_rows.astype(F32)).astype(BF16)
        near = jnp.concatenate(
            [(half1 + over1.astype(F32)).astype(BF16), (half3 + over3.astype(F32)).astype(BF16)]
        )
        keep0, send0 = chunks((0,), f02, lambda d: (0, 0), [send2, near])
        near = tie(swap(near, 1, "cuts"), keep0)
        over2 = tie(other_chip(send2), keep0)
        half0, send0 = to_chip(keep0, tie(send0, near, over2))
        near = near.astype(F32)
        sum2 = (half2 + over2.astype(F32) + near[tokens:]).astype(BF16)
        grads = adapter_back(low_x, low_g, gg, ug, h, [send0, sum2])
        grad_x, grad_down_out = factor_grads(tie(proj_all, sum2))
        far = tie(swap(sum2, 2, "cuts"), grads[0], grad_x, grad_down_out).astype(F32)
        over0 = other_chip(send0).astype(F32)
        input_grad = (half0 + over0 + near[:tokens] + far).astype(BF16)
    else:
        grads = adapter_back(low_x, low_g, gg, ug, h)
        dt = 768 if width % 768 == 0 else width
        at = jnp.arange(width // dt, dtype=jnp.int32)
        chunks = row_back(
            at, gg, ug, gate_proj, up_proj, back, proj, every_factor, lambda d: (0, d), dt
        )
        partial = jnp.concatenate(
            [jnp.concatenate(chunks[i : i + 2]) for i in range(0, len(chunks), 2)], axis=1
        )
        partial = lax.psum_scatter(partial, "expert", scatter_dimension=0, tiled=True)
        input_grad = lax.psum_scatter(partial, "cuts", scatter_dimension=1, tiled=True)
        grad_x, grad_down_out = factor_grads(lax.psum(proj.astype(F32), "cuts").astype(BF16))

    return (
        input_grad,
        grad_x[:, :rank],
        grads[0],
        grad_x[:, rank:],
        grads[1],
        grads[2],
        grad_down_out,
    )


def solution(mesh):
    return jax.shard_map(
        body,
        mesh=mesh,
        in_specs=(
            P(("parts", "expert"), "cuts"),
            P(("parts", "expert"), "cuts"),
            P(("parts", "expert"), None),
            P(("parts", "expert"), None),
            P("expert", None, "cuts"),
            P("expert", None, "cuts"),
            P("expert", "cuts", None),
            P("expert", None, "cuts"),
            P("expert", None, "cuts"),
            P("expert", None, "cuts"),
            P("expert", None, "cuts"),
            P("expert", None, "cuts"),
            P("expert", None, "cuts"),
        ),
        out_specs=(
            P(("parts", "expert"), "cuts"),
            P(("parts", "expert"), None, "cuts"),
            P(("parts", "expert"), None, "cuts"),
            P(("parts", "expert"), None, "cuts"),
            P(("parts", "expert"), None, "cuts"),
            P(("parts", "expert"), None, "cuts"),
            P(("parts", "expert"), None, "cuts"),
        ),
        check_vma=False,
    )
```
